32 devices in a mesh: groups: 2 (over x), dp: 8 (over z, y), layer: 2 (over core).
Axes of the slice: x: 2, y: 2, z: 4, core: 2. Of those that a mesh axis runs over, the one named last changes fastest.
Arguments:
- queries: bfloat16 [1024, 16384], P('dp', 'layer'), may hold values from -6 to 6
- documents: bfloat16 [10240, 16384], P(('groups', 'dp'), 'layer'), parts along dimension 0, may hold values from -6 to 6
- counts: int32 [16], P(('groups', 'dp')), parts along dimension 0, may hold values from 160 to 640, as said below
- eigenvalues: float32 [16384], P('layer'), may hold values from 0.05 to 20
Outputs:
- scores: float32 [10240, 384], P(('groups', 'dp', 'layer')), parts along dimension 0
The draws below stay inside these ranges and needn't reach their ends.
There are 2 independent parts, one for each index of `groups`. The reference program is written for one: setup_inputs(seed, part) draws one part's arguments, and reference() takes and returns one part's arrays. A program takes and returns all parts, laid end to end along the dimension named above; an argument that names none is the same for every part. Nothing has to cross between parts.
Inputs may be any that keep to these rules, and one draw needn't show every extreme that they name: `counts`: live document slots of each owner, filled from the first slot; at least one owner is full.
All inputs are finite; a program needn't handle non-finite values.
Results may differ from the reference program's by a relative error of at most 0.0029.
Values may be sent and summed in bfloat16 or wider, within the bound.
No kernel may reach another device: no remote copies, remote signals or barrier semaphores. Data moves between devices by JAX's collectives and lax.ppermute only.
A program may use at most 64 MiB of HBM per device.

```python
import math
import jax
import jax.numpy as jnp
from jax import lax

L_DIM = 8192
Q_DEV = 128
DOC_DEV = 640
WINDOW = 3
DIM = 16384
NQ = 1024
DOCS = 5120
N_DP = 8


def draw_counts(key, part):
    key = jax.random.fold_in(key, 7)
    first, second = jax.random.split(key)
    values = jax.random.randint(first, (N_DP,), DOC_DEV // 4, DOC_DEV + 1)
    chosen = jax.random.randint(second, (), 0, N_DP)
    return values.at[chosen].set(DOC_DEV).astype(jnp.int32)


def level_of(stream_key, dims, pieces, smallest, largest):
    gain, own = 1.0, jax.random.fold_in(stream_key, 6)
    for dim, parts in pieces:
        steps = jnp.exp(jax.random.uniform(jax.random.fold_in(own, dim), (parts,), jnp.float32, smallest / len(pieces), largest / len(pieces)))
        gain = gain * jnp.repeat(steps, dims[dim] // parts).reshape([-1 if axis == dim else 1 for axis in range(len(dims))])
    return gain


def centred(key, dims, deviation, limit, pieces=(), held_as=jnp.bfloat16):
    drawn = jax.random.normal(key, dims, jnp.float32) * deviation
    if len(pieces) > 0:
        drawn = level_of(key, dims, pieces, -0.22, 0.18) * drawn
    return jnp.clip(drawn, min=-limit, max=limit).astype(held_as)


def setup_inputs(seed: int = 0, part: int = 0) -> dict:
    seeds = jax.random.split(jax.random.key(seed), 5)
    part_keys = jax.random.split(jax.random.fold_in(seeds[4], part), 5)
    queries = centred(seeds[0], (NQ, DIM), 1.0, 6.0, ((0, 8), (1, 2)))
    documents = centred(part_keys[1], (DOCS, DIM), 1.0, 6.0, ((0, 8), (1, 2)))
    counts = draw_counts(jax.random.fold_in(jax.random.fold_in(seeds[4], part), 71), part)
    eigenvalues = jnp.clip(jnp.exp(math.log(20.0) - 5.9914645 * jax.random.uniform(seeds[3], (DIM,), jnp.float32) ** level_of(seeds[3], (DIM,), ((0, 2),), -0.2, 0.2)), 0.05, 20.0)
    return dict(queries=queries, documents=documents, counts=counts, eigenvalues=eigenvalues)


def reference(queries, documents, counts, eigenvalues):
    blocks = eigenvalues.reshape(-1, L_DIM)
    damping = 0.1 * lax.optimization_barrier(jnp.mean(blocks, axis=1, keepdims=True))
    inverse = (1.0 / (blocks + damping)).reshape(DIM)
    precond = (queries.astype(jnp.float32) * inverse).astype(jnp.bfloat16)
    query_blocks = precond.reshape(N_DP, Q_DEV, DIM)
    doc_blocks = documents.reshape(N_DP, DOC_DEV, DIM)
    factor = 1.0 / jnp.sqrt(jnp.float32(DIM))

    def owner_scores(owner):
        docs_here = doc_blocks[owner]
        columns = []
        for slot in range(WINDOW):
            source = jnp.mod(owner - slot, N_DP).astype(jnp.int32)
            block = query_blocks[source]
            columns.append(lax.dot_general(docs_here, block, (((1,), (1,)), ((), ())), preferred_element_type=jnp.float32))
        joined = jnp.concatenate(columns, axis=1) * factor
        live = (jnp.arange(DOC_DEV, dtype=jnp.int32) < counts[owner]).astype(jnp.float32)
        return joined * live[:, None]
    result = lax.map(owner_scores, jnp.arange(N_DP, dtype=jnp.int32))
    return result.reshape(DOCS, WINDOW * Q_DEV)
```

```python
import functools
import math

import jax
import jax.numpy as jnp
from jax import lax
from jax.experimental import pallas as pl
from jax.experimental.pallas import tpu as pltpu
from jax.sharding import PartitionSpec as P

L_DIM = 8192
CHUNKS = 8
PHASES = 6


def score_kernel(count, targets, fresh, where_ref, documents, inverse, *refs):
    blocks = max(targets) + 1
    chunks, refs = refs[:count], refs[count:]
    if fresh:
        sums, refs = None, refs
    else:
        sums, refs = refs[0], refs[1:]
    out, rows_buf, sem = refs
    half = documents.shape[0] // 2
    width = chunks[0].shape[1]
    layer = where_ref[count]

    def copies(i):
        column = pl.multiple_of(where_ref[i] * width, width)
        return [
            pltpu.make_async_copy(
                documents.at[
                    pl.ds(pl.multiple_of(row * half, half), half), pl.ds(column, width)
                ],
                rows_buf.at[i, pl.ds(place * half, half), :],
                sem.at[i, place],
            )
            for place, row in enumerate((1 - layer, layer))
        ]

    for i in range(count):
        for copy in copies(i):
            copy.start()
    for b in range(blocks):
        out[b] = jnp.zeros_like(out[b]) if fresh else sums[b]
    for i in range(count):
        for copy in copies(i):
            copy.wait()
        scaled = chunks[i][...].astype(jnp.float32) * inverse[where_ref[i]]
        out[targets[i]] += lax.dot_general(
            rows_buf[i],
            scaled.astype(jnp.bfloat16),
            (((1,), (1,)), ((), ())),
            preferred_element_type=jnp.float32,
        )


def add_scores(documents, inverse, layer, chunks, places, targets, sums=None):
    count = len(chunks)
    blocks = max(targets) + 1
    doc_rows = documents.shape[0]
    rows, width = chunks[0].shape
    where = jnp.stack([jnp.asarray(p, jnp.int32) for p in places] + [layer])
    vmem = pl.BlockSpec(memory_space=pltpu.VMEM)
    operands = [where, documents, inverse, *chunks]
    specs = [pl.BlockSpec(memory_space=pltpu.SMEM), pl.BlockSpec(memory_space=pl.ANY)]
    specs += [vmem] * (1 + count)
    if sums is not None:
        operands.append(sums)
        specs.append(vmem)
    return pl.pallas_call(
        functools.partial(score_kernel, count, targets, sums is None),
        out_shape=jax.ShapeDtypeStruct((blocks, doc_rows, rows), jnp.float32),
        in_specs=specs,
        out_specs=vmem,
        scratch_shapes=[
            pltpu.VMEM((count, doc_rows, width), documents.dtype),
            pltpu.SemaphoreType.DMA((count, 2)),
        ],
        compiler_params=pltpu.CompilerParams(vmem_limit_bytes=40 * 1024 * 1024),
        cost_estimate=pl.CostEstimate(
            flops=2 * count * doc_rows * rows * width,
            bytes_accessed=count * doc_rows * width * 2,
            transcendentals=0,
        ),
    )(*operands)


def on_device(queries, documents, counts, eigenvalues):
    dim_here = eigenvalues.shape[0]
    owners = lax.axis_size("dp")
    rows = queries.shape[0]
    doc_rows = documents.shape[0]
    half = doc_rows // 2
    width = dim_here // CHUNKS
    group, owner, layer = (lax.axis_index(a).astype(jnp.int32) for a in ("groups", "dp", "layer"))
    even = owner % 2 == 0

    def place(k):
        return jnp.where(group == 0, k, CHUNKS - 1 - k).astype(jnp.int32)

    own = [
        lax.dynamic_slice(queries, (0, place(k) * width), (rows, width)) for k in range(PHASES)
    ]
    ahead = [(i, (i + 2) % owners) for i in range(owners)]
    up = [(i, i + 1) for i in range(0, owners, 2)]
    down = [(i + 1, i) for i in range(0, owners, 2)]
    across = [(0, 1), (1, 0)]

    far, near, far_across, near_across = [], [], [], []
    for p in range(PHASES):
        far.append(lax.ppermute(own[p], "dp", ahead))
        if p == 0:
            near.append(lax.ppermute(own[0], "dp", up))
        elif p < PHASES - 1:
            near.append(lax.ppermute(jnp.where(even, own[p], far[p - 1]), "dp", up + down))
        else:
            near.append(lax.ppermute(far[p - 1], "dp", down))
        if p in (1, 3):
            far_across.append(lax.ppermute(far[(p - 1) // 2], "groups", across))
        elif p >= 2:
            k = {2: 0, 4: 1, 5: 2}[p]
            near_across.append(
                lax.ppermute(jnp.where(even, near[k + 1], near[k]), "groups", across)
            )

    blocks = eigenvalues.reshape(dim_here // L_DIM, L_DIM)
    damping = 0.1 * jnp.mean(blocks, axis=1, keepdims=True)
    inverse = (1.0 / (blocks + damping)).reshape(CHUNKS, 1, width)

    run = functools.partial(add_scores, documents, inverse, layer)
    mine0 = run(
        [queries[:, k * width : (k + 1) * width] for k in range(CHUNKS)],
        list(range(CHUNKS)),
        [0] * CHUNKS,
    )
    got0 = lax.ppermute(mine0[0, :half], "layer", across)

    near_k = [jnp.where(even, near[k + 1], near[k]) for k in range(PHASES - 1)]
    first = run(
        [far[0], far[1], far[2], near_k[0], near_k[1], far_across[0], near_across[0]],
        [place(0), place(1), place(2), place(0), place(1), place(CHUNKS - 1), place(CHUNKS - 1)],
        [1, 1, 1, 0, 0, 1, 0],
    )
    second = run(
        [far[3], far[4], near_k[2], near_k[3], far_across[1], near_across[1]],
        [place(3), place(4), place(2), place(3), place(CHUNKS - 2), place(CHUNKS - 2)],
        [1, 1, 0, 0, 1, 0],
        first,
    )
    last = run(
        [far[5], near_k[4], near_across[2]],
        [place(5), place(4), place(CHUNKS - 3)],
        [1, 0, 0],
        second,
    )
    got12 = lax.ppermute(last[:, :half], "layer", across)
    factor = 1.0 / math.sqrt(dim_here * lax.axis_size("layer"))
    doc_index = layer * half + jnp.arange(half, dtype=jnp.int32)
    scale = (factor * (doc_index < counts[0]).astype(jnp.float32))[:, None]
    both = last[:, half:] + got12
    return jnp.concatenate([mine0[0, half:] + got0, both[0], both[1]], axis=1) * scale


def solution(mesh):
    return jax.shard_map(
        on_device,
        mesh=mesh,
        in_specs=(P("dp", "layer"), P(("groups", "dp"), "layer"), P(("groups", "dp")), P("layer")),
        out_specs=P(("groups", "dp", "layer"), None),
        check_vma=False,
    )
```

```python
import functools
import math

import jax
import jax.numpy as jnp
from jax import lax
from jax.experimental import pallas as pl
from jax.experimental.pallas import tpu as pltpu
from jax.sharding import PartitionSpec as P

L_DIM = 8192
CHUNKS = 8
DIRECT = 6
VMEM = pl.BlockSpec(memory_space=pltpu.VMEM)
SMEM = pl.BlockSpec(memory_space=pltpu.SMEM)
ANY = pl.BlockSpec(memory_space=pl.ANY)
SMALL = pl.CostEstimate(flops=1024, bytes_accessed=1024, transcendentals=0)
PARAMS = pltpu.CompilerParams(vmem_limit_bytes=24 * 1024 * 1024)


def columns_of(k, width):
    place = jnp.where(lax.axis_index("groups") == 0, k, CHUNKS - 1 - k)
    return pl.ds(pl.multiple_of(place * width, width), width)


def document_copies(documents, rows_buf, sem, slot, columns, sides):
    layer = lax.axis_index("layer")
    half = documents.shape[0] // 2
    copies = []
    for at, side in enumerate(sides):
        row = layer if side else 1 - layer
        copies.append(
            pltpu.make_async_copy(
                documents.at[pl.ds(pl.multiple_of(row * half, half), half), columns],
                rows_buf.at[slot, pl.ds(at * half, half), :],
                sem.at[slot, at],
            )
        )
    return copies


def products(rows, block):
    return lax.dot_general(
        rows, block, (((1,), (1,)), ((), ())), preferred_element_type=jnp.float32
    )


def first_kernel(count, queries, *refs):
    outs, sem = refs[:count], refs[count]
    width = outs[0].shape[1]
    copies = [
        pltpu.make_async_copy(queries.at[:, columns_of(k, width)], outs[k], sem.at[k])
        for k in range(count)
    ]
    for copy in copies:
        copy.start()
    for copy in copies:
        copy.wait()


def step_kernel(k, ahead, queries, received, *refs):
    outs, sem = refs[-2 - (ahead is not None) : -1], refs[-1]
    width = received.shape[1]
    even = lax.axis_index("dp") % 2 == 0
    own_copy = pltpu.make_async_copy(queries.at[:, columns_of(k, width)], outs[0], sem.at[0])
    received_copy = pltpu.make_async_copy(received, outs[0], sem.at[0])
    if ahead is not None:
        ahead_copy = pltpu.make_async_copy(
            queries.at[:, columns_of(ahead, width)], outs[1], sem.at[1]
        )
        ahead_copy.start()

    @pl.when(even)
    def _():
        own_copy.start()
        own_copy.wait()

    @pl.when(jnp.logical_not(even))
    def _():
        received_copy.start()
        received_copy.wait()

    if ahead is not None:
        ahead_copy.wait()


def own_kernel(part, held, documents, queries, *refs):
    if part == 0:
        eigenvalues = refs[0]
        theirs, mine, inverse, rows_buf, sem = refs[1 + held :]
    else:
        inverse, theirs_sum, mine_sum = refs[:3]
        theirs, mine, rows_buf, sem = refs[3 + held :]
    half = documents.shape[0] // 2
    count, _, width = rows_buf.shape
    copies = []
    for i in range(count):
        k = part * count + i
        copies.append(
            document_copies(documents, rows_buf, sem, i, pl.ds(k * width, width), (0, 1))
        )
        for copy in copies[i]:
            copy.start()
    if part == 0:
        for start in range(0, eigenvalues.shape[1], L_DIM):
            block = eigenvalues[:, start : start + L_DIM]
            damping = 0.1 * jnp.mean(block, axis=1, keepdims=True)
            inverse[:, start : start + L_DIM] = 1.0 / (block + damping)
    for i in range(count):
        k = part * count + i
        scaled = queries[:, i * width : (i + 1) * width].astype(jnp.float32)
        scaled = (scaled * inverse[:, k * width : (k + 1) * width]).astype(jnp.bfloat16)
        for copy in copies[i]:
            copy.wait()
        term = products(rows_buf[i], scaled)
        if i > 0:
            theirs[...] += term[:half]
            mine[...] += term[half:]
        elif part == 0:
            theirs[...] = term[:half]
            mine[...] = term[half:]
        else:
            theirs[...] = theirs_sum[...] + term[:half]
            mine[...] = mine_sum[...] + term[half:]


def pair_kernel(ks, sides, fresh, documents, inverse, *refs):
    count = len(ks)
    chunks, refs = refs[: 2 * count], refs[2 * count :]
    if not fresh:
        sums = refs[0]
    out, rows_buf, block_buf, sem = refs[-4:]
    half = documents.shape[0] // 2
    first = 0 if 0 in sides else half
    rows, width = chunks[0].shape
    columns = [columns_of(k, width) for k in ks]
    copies = [
        document_copies(documents, rows_buf, sem, i, columns[i], sides) for i in range(count)
    ]
    for pair in copies:
        for copy in pair:
            copy.start()
    for i in range(count):
        for b in range(2):
            scaled = chunks[2 * i + b][...].astype(jnp.float32) * inverse[:, columns[i]]
            block_buf[i, pl.ds(b * rows, rows), :] = scaled.astype(jnp.bfloat16)
        for copy in copies[i]:
            copy.wait()
        term = products(rows_buf[i], block_buf[i])
        if i > 0:
            out[...] += term
        elif fresh:
            out[...] = term
        else:
            out[...] = sums[pl.ds(first, out.shape[0]), :] + term


def final_kernel(factor, counts, mine0, got0, mine, got, out):
    half, rows = mine0.shape
    start = lax.axis_index("layer") * half
    index = start + lax.broadcasted_iota(jnp.int32, (half, 1), 0)
    scale = factor * (index < counts[0]).astype(jnp.float32)
    out[:, :rows] = (mine0[...] + got0[...]) * scale
    out[:, rows:] = (mine[...] + got[...]) * scale


def on_device(queries, documents, counts, eigenvalues):
    rows, dims = queries.shape
    doc_rows = documents.shape[0]
    half = doc_rows // 2
    owners = lax.axis_size("dp")
    width = dims // CHUNKS
    ahead = [(i, (i + 2) % owners) for i in range(owners)]
    pair = [(i, i ^ 1) for i in range(owners)]
    across = [(0, 1), (1, 0)]
    chunk = jax.ShapeDtypeStruct((rows, width), queries.dtype)

    def call(kernel, out_shape, in_specs, out_specs, scratch):
        return pl.pallas_call(
            kernel,
            out_shape=out_shape,
            in_specs=in_specs,
            out_specs=out_specs,
            scratch_shapes=scratch,
            compiler_params=PARAMS,
            cost_estimate=SMALL,
        )

    def step(k, *until):
        ahead_k = k + 2 if k + 2 < DIRECT else None
        outs = 1 if ahead_k is None else 2
        return call(
            functools.partial(step_kernel, k, ahead_k),
            [chunk] * outs,
            [ANY] * (2 + len(until)),
            [ANY] * outs,
            [pltpu.SemaphoreType.DMA((2,))],
        )(queries, far[k], *until)

    def own_scores(part, *operands, until=()):
        half_scores = jax.ShapeDtypeStruct((half, rows), jnp.float32)
        outs = [half_scores] * 2
        if part == 0:
            outs.append(jax.ShapeDtypeStruct((1, dims), jnp.float32))
        return pl.pallas_call(
            functools.partial(own_kernel, part, len(until)),
            out_shape=outs,
            grid=(1,),
            in_specs=[ANY, pl.BlockSpec((rows, dims // 2), lambda i: (0, part))]
            + [VMEM] * len(operands)
            + [ANY] * len(until),
            out_specs=[VMEM] * len(outs),
            scratch_shapes=[
                pltpu.VMEM((CHUNKS // 2, doc_rows, width), documents.dtype),
                pltpu.SemaphoreType.DMA((CHUNKS // 2, 2)),
            ],
            compiler_params=PARAMS,
            cost_estimate=SMALL,
        )(documents, queries, *operands, *until)

    def pair_scores(*ks, sums=None, sides=(0, 1), until=()):
        count = len(ks)
        side_rows = half * len(sides)
        operands = [inverse] + [block[k] for k in ks for block in (near, far)]
        if sums is not None:
            operands.append(sums)
        return call(
            functools.partial(pair_kernel, ks, sides, sums is None),
            jax.ShapeDtypeStruct((side_rows, 2 * rows), jnp.float32),
            [ANY] + [VMEM] * len(operands) + [ANY] * len(until),
            VMEM,
            [
                pltpu.VMEM((count, side_rows, width), documents.dtype),
                pltpu.VMEM((count, 2 * rows, width), documents.dtype),
                pltpu.SemaphoreType.DMA((count, len(sides))),
            ],
        )(documents, *operands, *until)

    far = [None] * CHUNKS
    near = [None] * CHUNKS

    def send_across(block, k, *until):
        sent = lax.optimization_barrier((block[k], *until))[0]
        block[CHUNKS - 1 - k] = lax.ppermute(sent, "groups", across)

    def send(k, outs):
        near[k] = lax.ppermute(outs[0], "dp", pair)
        if len(outs) > 1:
            far[k + 2] = lax.ppermute(outs[1], "dp", ahead)

    for k, to_send in enumerate(
        call(
            functools.partial(first_kernel, 2),
            [chunk] * 2,
            [ANY],
            [ANY] * 2,
            [pltpu.SemaphoreType.DMA((2,))],
        )(queries)
    ):
        far[k] = lax.ppermute(to_send, "dp", ahead)
    theirs0, mine0, inverse = own_scores(0, eigenvalues.reshape(1, dims), until=(to_send,))

    outs = step(0, inverse)
    send(0, outs)
    send_across(far, 0, outs[0])
    theirs0, mine0 = own_scores(1, inverse, theirs0, mine0, until=(outs[0],))

    outs = step(1, theirs0)
    send(1, outs)
    send_across(far, 1, outs[0])
    sums = pair_scores(0, until=(outs[0], far[CHUNKS - 1]))

    outs = step(2, sums)
    send(2, outs)
    send_across(near, 0, outs[0])
    sums = pair_scores(1, sums=sums, until=(outs[0], far[CHUNKS - 2]))

    outs = step(3, sums)
    send(3, outs)
    send_across(near, 1, outs[0])
    sums = pair_scores(2, CHUNKS - 1, sums=sums, until=(outs[0],))

    outs = step(4, sums)
    send(4, outs)
    send_across(near, 2, outs[0])
    sent0 = lax.optimization_barrier((theirs0, outs[0]))[0]
    got0 = lax.ppermute(sent0, "layer", across)
    sums = pair_scores(3, CHUNKS - 2, sums=sums, until=(outs[0],))
    theirs = pair_scores(4, 5, sums=sums, sides=(0,), until=(got0,))
    got = lax.ppermute(theirs, "layer", across)
    mine = pair_scores(4, 5, sums=sums, sides=(1,), until=(theirs,))
    factor = 1.0 / math.sqrt(dims * lax.axis_size("layer"))
    return call(
        functools.partial(final_kernel, factor),
        jax.ShapeDtypeStruct((half, 3 * rows), jnp.float32),
        [SMEM] + [VMEM] * 4,
        VMEM,
        [],
    )(counts, mine0, got0, mine, got)


def solution(mesh):
    return jax.shard_map(
        on_device,
        mesh=mesh,
        in_specs=(P("dp", "layer"), P(("groups", "dp"), "layer"), P(("groups", "dp")), P("layer")),
        out_specs=P(("groups", "dp", "layer"), None),
        check_vma=False,
    )
```

```python
import functools
import math

import jax
import jax.numpy as jnp
from jax import lax
from jax.experimental import pallas as pl
from jax.experimental.pallas import tpu as pltpu
from jax.sharding import PartitionSpec as P

L_DIM = 8192
SIZES = (8, 8, 8, 8, 8, 8, 8, 8)
CHUNKS = len(SIZES)
AHEAD = 6
VMEM = pl.BlockSpec(memory_space=pltpu.VMEM)
SMEM = pl.BlockSpec(memory_space=pltpu.SMEM)
HBM = pl.BlockSpec(memory_space=pltpu.HBM)
ANY = pl.BlockSpec(memory_space=pl.ANY)
SMALL = pl.CostEstimate(flops=1024, bytes_accessed=1024, transcendentals=0)
MIB = 1024 * 1024


def width_of(k, dims):
    return SIZES[k] * dims // sum(SIZES)


def columns_of(k, dims):
    unit = dims // sum(SIZES)
    start = jnp.where(
        lax.axis_index("groups") == 0, sum(SIZES[:k]) * unit, sum(SIZES[k + 1 :]) * unit
    )
    return pl.ds(pl.multiple_of(start, unit), width_of(k, dims))


def products(rows, block):
    return lax.dot_general(
        rows, block, (((1,), (1,)), ((), ())), preferred_element_type=jnp.float32
    )


def scale_of(factor, counts, half, side):
    layer = lax.axis_index("layer")
    start = (layer if side else 1 - layer) * half
    index = start + lax.broadcasted_iota(jnp.int32, (half, 1), 0)
    return factor * (index < counts[0]).astype(jnp.float32)


def first_kernel(queries, *refs):
    outs, sem = refs[:2], refs[2]
    dims = queries.shape[1]
    copies = [
        pltpu.make_async_copy(queries.at[:, columns_of(k, dims)], outs[k], sem.at[k])
        for k in range(2)
    ]
    for copy in copies:
        copy.start()
    for copy in copies:
        copy.wait()


def step_kernel(k, ahead, queries, received, *refs):
    outs, sem = refs[-2 - (ahead is not None) : -1], refs[-1]
    dims = queries.shape[1]
    even = lax.axis_index("dp") % 2 == 0
    own_copy = pltpu.make_async_copy(queries.at[:, columns_of(k, dims)], outs[0], sem.at[0])
    received_copy = pltpu.make_async_copy(received, outs[0], sem.at[0])
    if ahead is not None:
        ahead_copy = pltpu.make_async_copy(
            queries.at[:, columns_of(ahead, dims)], outs[1], sem.at[1]
        )
        ahead_copy.start()

    @pl.when(even)
    def _():
        own_copy.start()
        own_copy.wait()

    @pl.when(jnp.logical_not(even))
    def _():
        received_copy.start()
        received_copy.wait()

    if ahead is not None:
        ahead_copy.wait()


def own_kernel(factor, pieces, counts, documents, queries, eigenvalues, *refs):
    theirs, mine, inverse, held, own, doc_sem, own_sem = refs[-7:]
    layer = lax.axis_index("layer")
    half = documents.shape[0] // 2
    dims = documents.shape[1]
    width = dims // pieces
    copies = []
    for i in range(pieces):
        columns = pl.ds(i * width, width)
        copies.append([pltpu.make_async_copy(queries.at[:, columns], own.at[:, columns], own_sem.at[i])])
        for at, row in enumerate((1 - layer, layer)):
            copies[i].append(
                pltpu.make_async_copy(
                    documents.at[pl.ds(pl.multiple_of(row * half, half), half), columns],
                    held.at[pl.ds(at * half, half), columns],
                    doc_sem.at[i, at],
                )
            )
        for copy in copies[i]:
            copy.start()
    for start in range(0, dims, L_DIM):
        block = eigenvalues[:, start : start + L_DIM]
        damping = 0.1 * jnp.mean(block, axis=1, keepdims=True)
        inverse[:, start : start + L_DIM] = 1.0 / (block + damping)
    for i in range(pieces):
        for copy in copies[i]:
            copy.wait()
        columns = slice(i * width, (i + 1) * width)
        scaled = (own[:, columns].astype(jnp.float32) * inverse[:, columns]).astype(jnp.bfloat16)
        for out, rows in ((theirs, slice(0, half)), (mine, slice(half, 2 * half))):
            term = products(held[rows, columns], scaled)
            if i == 0:
                out[...] = term
            else:
                out[...] += term
    theirs[...] *= scale_of(factor, counts, half, 0)
    mine[...] *= scale_of(factor, counts, half, 1)


def pair_kernel(ks, side, factor, fresh, counts, held, inverse, *refs):
    count = len(ks)
    chunks, refs = refs[: 2 * count], refs[2 * count :]
    if not fresh:
        sums = refs[0]
    out, block_buf = refs[-2:]
    dims = held.shape[1]
    first = 0 if side is None else side * out.shape[0]
    rows = chunks[0].shape[0]
    for i, k in enumerate(ks):
        columns = columns_of(k, dims)
        width = width_of(k, dims)
        for b in range(2):
            scaled = chunks[2 * i + b][...].astype(jnp.float32) * inverse[:, columns]
            block_buf[pl.ds(b * rows, rows), :width] = scaled.astype(jnp.bfloat16)
        term = products(held[pl.ds(first, out.shape[0]), columns], block_buf[:, :width])
        if i > 0:
            out[...] += term
        elif fresh:
            out[...] = term
        else:
            out[...] = sums[pl.ds(first, out.shape[0]), :] + term
    if side is not None:
        out[...] *= scale_of(factor, counts, out.shape[0], side)


def final_kernel(mine0, got0, mine, got, out):
    rows = mine0.shape[1]
    out[:, :rows] = mine0[...] + got0[...]
    out[:, rows:] = mine[...] + got[...]


def on_device(queries, documents, counts, eigenvalues):
    rows, dims = queries.shape
    doc_rows = documents.shape[0]
    half = doc_rows // 2
    owners = lax.axis_size("dp")
    factor = 1.0 / math.sqrt(dims * lax.axis_size("layer"))
    ahead = [(i, (i + 2) % owners) for i in range(owners)]
    pair = [(i, i ^ 1) for i in range(owners)]
    across = [(0, 1), (1, 0)]

    def chunk(k):
        return jax.ShapeDtypeStruct((rows, width_of(k, dims)), queries.dtype)

    def scores(count):
        return jax.ShapeDtypeStruct((count, 2 * rows), jnp.float32)

    def call(kernel, out_shape, in_specs, out_specs, scratch, vmem_mib=16):
        return pl.pallas_call(
            kernel,
            out_shape=out_shape,
            in_specs=in_specs,
            out_specs=out_specs,
            scratch_shapes=scratch,
            compiler_params=pltpu.CompilerParams(vmem_limit_bytes=vmem_mib * MIB),
            cost_estimate=SMALL,
        )

    def step(k, *until):
        ahead_k = k + 2 if k + 2 < AHEAD else None
        outs = [chunk(k)] + ([] if ahead_k is None else [chunk(ahead_k)])
        return call(
            functools.partial(step_kernel, k, ahead_k),
            outs,
            [HBM, ANY] + [ANY] * len(until),
            [ANY] * len(outs),
            [pltpu.SemaphoreType.DMA((2,))],
        )(queries, far[k], *until)

    def pair_scores(*ks, sums=None, side=None, until=()):
        operands = [held, inverse] + [block[k] for k in ks for block in (near, far)]
        if sums is not None:
            operands.append(sums)
        return call(
            functools.partial(pair_kernel, ks, side, factor, sums is None),
            scores(doc_rows if side is None else half),
            [SMEM] + [VMEM] * len(operands) + [ANY] * len(until),
            VMEM,
            [pltpu.VMEM((2 * rows, max(width_of(k, dims) for k in ks)), queries.dtype)],
        )(counts, *operands, *until)

    far = [None] * CHUNKS
    near = [None] * CHUNKS

    def send_across(block, k, *until):
        sent = lax.optimization_barrier((block[k], *until))[0]
        block[CHUNKS - 1 - k] = lax.ppermute(sent, "groups", across)

    def send(k, outs):
        near[k] = lax.ppermute(outs[0], "dp", pair)
        if len(outs) > 1:
            far[k + 2] = lax.ppermute(outs[1], "dp", ahead)

    sent = call(
        first_kernel,
        [chunk(0), chunk(1)],
        [HBM],
        [ANY] * 2,
        [pltpu.SemaphoreType.DMA((2,))],
        vmem_mib=60,
    )(queries)
    for k in range(2):
        far[k] = lax.ppermute(sent[k], "dp", ahead)
    pieces = 8
    theirs0, mine0, inverse, held = call(
        functools.partial(own_kernel, factor, pieces),
        [
            jax.ShapeDtypeStruct((half, rows), jnp.float32),
            jax.ShapeDtypeStruct((half, rows), jnp.float32),
            jax.ShapeDtypeStruct((1, dims), jnp.float32),
            jax.ShapeDtypeStruct(documents.shape, documents.dtype),
        ],
        [SMEM, HBM, HBM, VMEM],
        [VMEM] * 4,
        [
            pltpu.VMEM((rows, dims), queries.dtype),
            pltpu.SemaphoreType.DMA((pieces, 2)),
            pltpu.SemaphoreType.DMA((pieces,)),
        ],
        vmem_mib=40,
    )(counts, documents, queries, lax.optimization_barrier((eigenvalues, sent[1]))[0].reshape(1, dims))

    outs = step(0, inverse)
    send(0, outs)
    send_across(far, 0, outs[0])

    outs = step(1)
    send(1, outs)
    send_across(far, 1, outs[0])
    sums = pair_scores(0, until=(outs[0], far[CHUNKS - 1]))

    outs = step(2, sums)
    send(2, outs)
    send_across(near, 0, outs[0])
    sums = pair_scores(1, sums=sums, until=(outs[0], far[CHUNKS - 2]))

    outs = step(3, sums)
    send(3, outs)
    send_across(near, 1, outs[0])
    sums = pair_scores(2, CHUNKS - 1, sums=sums, until=(outs[0],))

    outs = step(4, sums)
    send(4, outs)
    send_across(near, 2, outs[0])
    sent0 = lax.optimization_barrier((theirs0, outs[0]))[0]
    got0 = lax.ppermute(sent0, "layer", across)
    sums = pair_scores(3, CHUNKS - 2, sums=sums, until=(outs[0],))
    theirs = pair_scores(4, 5, sums=sums, side=0, until=(got0,))
    got = lax.ppermute(theirs, "layer", across)
    mine = pair_scores(4, 5, sums=sums, side=1, until=(theirs,))
    return call(final_kernel, jax.ShapeDtypeStruct((half, 3 * rows), jnp.float32), [VMEM] * 4, VMEM, [])(
        mine0, got0, mine, got
    )


def solution(mesh):
    return jax.shard_map(
        on_device,
        mesh=mesh,
        in_specs=(P("dp", "layer"), P(("groups", "dp"), "layer"), P(("groups", "dp")), P("layer")),
        out_specs=P(("groups", "dp", "layer"), None),
        check_vma=False,
    )
```

```python
import functools
import math

import jax
import jax.numpy as jnp
from jax import lax
from jax.experimental import pallas as pl
from jax.experimental.pallas import tpu as pltpu
from jax.sharding import PartitionSpec as P

L_DIM = 8192
SIZES = (12, 12, 8, 8, 12, 12)
CHUNKS = len(SIZES)
DIRECT = 5
OWN_MIB = (44, 40)
VMEM = pl.BlockSpec(memory_space=pltpu.VMEM)
SMEM = pl.BlockSpec(memory_space=pltpu.SMEM)
HBM = pl.BlockSpec(memory_space=pltpu.HBM)
ANY = pl.BlockSpec(memory_space=pl.ANY)
COST = pl.CostEstimate(flops=2 * 10**9, bytes_accessed=0, transcendentals=0)
MIB = 1024 * 1024


def width_of(k, dims):
    return SIZES[k] * dims // sum(SIZES)


def columns_of(k, dims, within=None):
    unit = dims // sum(SIZES)
    left, right = sum(SIZES[:k]), sum(SIZES[k + 1 :])
    if within:
        left, right = left % (sum(SIZES) // 2), right % (sum(SIZES) // 2)
    start = jnp.where(lax.axis_index("groups") == 0, left * unit, right * unit)
    return pl.ds(pl.multiple_of(start, unit), width_of(k, dims))


def half_columns(part, dims):
    group = lax.axis_index("groups")
    side = group if part == 0 else 1 - group
    return pl.ds(pl.multiple_of(side * (dims // 2), dims // 2), dims // 2)


def products(rows, block):
    return lax.dot_general(
        rows, block, (((1,), (1,)), ((), ())), preferred_element_type=jnp.float32
    )


def scale_of(factor, counts, half, side):
    layer = lax.axis_index("layer")
    start = (layer if side else 1 - layer) * half
    index = start + lax.broadcasted_iota(jnp.int32, (half, 1), 0)
    return factor * (index < counts[0]).astype(jnp.float32)


def chunk_kernel(ks, queries, *refs):
    outs, sem = refs[-len(ks) - 1 : -1], refs[-1]
    dims = queries.shape[1]
    copies = [
        pltpu.make_async_copy(queries.at[:, columns_of(k, dims)], outs[i], sem.at[i])
        for i, k in enumerate(ks)
    ]
    for copy in copies:
        copy.start()
    for copy in copies:
        copy.wait()


def step_kernel(k, queries, received, *refs):
    out, sem = refs[-2:]
    even = lax.axis_index("dp") % 2 == 0
    own_copy = pltpu.make_async_copy(queries.at[:, columns_of(k, queries.shape[1])], out, sem)
    received_copy = pltpu.make_async_copy(received, out, sem)

    @pl.when(even)
    def _():
        own_copy.start()
        own_copy.wait()

    @pl.when(jnp.logical_not(even))
    def _():
        received_copy.start()
        received_copy.wait()


def own_kernel(part, pieces, documents, queries, *refs):
    if part == 0:
        eigenvalues, sums, held, inverse, sem = refs[0], *refs[-4:]
    else:
        inverse, before, sums, held, sem = refs[0], refs[1], *refs[-3:]
    layer = lax.axis_index("layer")
    half = documents.shape[0] // 2
    dims = documents.shape[1]
    width = dims // 2 // pieces
    first = half_columns(part, dims).start
    copies = []
    for i in range(pieces):
        start = pl.multiple_of(first + i * width, width)
        for at, row in enumerate((1 - layer, layer)):
            copies.append(
                pltpu.make_async_copy(
                    documents.at[pl.ds(pl.multiple_of(row * half, half), half), pl.ds(start, width)],
                    held.at[pl.ds(at * half, half), pl.ds(i * width, width)],
                    sem.at[i, at],
                )
            )
    for copy in copies:
        copy.start()
    if part == 0:
        for start in range(0, dims, L_DIM):
            block = eigenvalues[:, start : start + L_DIM]
            damping = 0.1 * jnp.mean(block, axis=1, keepdims=True)
            inverse[:, start : start + L_DIM] = 1.0 / (block + damping)
    for i in range(pieces):
        columns = pl.ds(pl.multiple_of(first + i * width, width), width)
        scaled = (queries[:, columns].astype(jnp.float32) * inverse[:, columns]).astype(jnp.bfloat16)
        copies[2 * i].wait()
        copies[2 * i + 1].wait()
        term = products(held[:, i * width : (i + 1) * width], scaled)
        if i > 0:
            sums[...] += term
        elif part == 0:
            sums[...] = term
        else:
            sums[...] = before[...] + term


def held_of(k, held):
    return held[0] if k < CHUNKS // 2 else held[1]


def add_pairs(ks, fresh, held, inverse, chunks, sums, out, block_buf):
    dims = inverse.shape[1]
    rows = chunks[0].shape[0]
    for i, k in enumerate(ks):
        width = width_of(k, dims)
        for b in range(2):
            scaled = chunks[2 * i + b][...].astype(jnp.float32) * inverse[:, columns_of(k, dims)]
            block_buf[pl.ds(b * rows, rows), :width] = scaled.astype(jnp.bfloat16)
        term = products(held_of(k, held)[:, columns_of(k, dims, True)], block_buf[:, :width])
        if i > 0:
            out[...] += term
        elif fresh:
            out[...] = term
        else:
            out[...] = sums[...] + term


def one_product(k, rows, held, inverse, chunk):
    dims = inverse.shape[1]
    scaled = chunk[...].astype(jnp.float32) * inverse[:, columns_of(k, dims)]
    return products(held_of(k, held)[rows, columns_of(k, dims, True)], scaled.astype(jnp.bfloat16))


def pair_kernel(ks, fresh, held0, held1, inverse, *refs):
    chunks = refs[: 2 * len(ks)]
    add_pairs(ks, fresh, (held0, held1), inverse, chunks, refs[2 * len(ks)], refs[-2], refs[-1])


def far_kernel(ks, k, factor, counts, held0, held1, inverse, *refs):
    held = held0, held1
    count = 2 * len(ks)
    chunks, (last, sums, own), (near, theirs, mine, total, block_buf) = (
        refs[:count],
        refs[count : count + 3],
        refs[count + 3 :],
    )
    rows = last.shape[0]
    half = mine.shape[0]
    add_pairs(ks, False, held, inverse, chunks, sums, total, block_buf)
    near[...] = total[:, :rows]
    far = total[:, rows:] + one_product(k, slice(None), held, inverse, last)
    for side, out in enumerate((theirs, mine)):
        scale = scale_of(factor, counts, half, side)
        out[:, :rows] = own[side * half : (side + 1) * half] * scale
        out[:, rows:] = far[side * half : (side + 1) * half] * scale


def near_kernel(k, side, factor, counts, held0, held1, inverse, last, near, *refs):
    out = refs[-1]
    half = out.shape[0]
    rows = slice(side * half, (side + 1) * half)
    total = near[rows] + one_product(k, rows, (held0, held1), inverse, last)
    out[...] = total * scale_of(factor, counts, half, side)


def final_kernel(mine, got, mine_near, got_near, out):
    rows = mine_near.shape[1]
    out[:, :rows] = mine[:, :rows] + got[:, :rows]
    out[:, rows : 2 * rows] = mine_near[...] + got_near[...]
    out[:, 2 * rows :] = mine[:, rows:] + got[:, rows:]


def on_device(queries, documents, counts, eigenvalues):
    rows, dims = queries.shape
    doc_rows = documents.shape[0]
    half = doc_rows // 2
    owners = lax.axis_size("dp")
    factor = 1.0 / math.sqrt(dims * lax.axis_size("layer"))
    ahead = [(i, (i + 2) % owners) for i in range(owners)]
    pair = [(i, i ^ 1) for i in range(owners)]
    across = [(0, 1), (1, 0)]

    def chunk(k):
        return jax.ShapeDtypeStruct((rows, width_of(k, dims)), queries.dtype)

    def floats(*shape):
        return jax.ShapeDtypeStruct(shape, jnp.float32)

    def call(kernel, out_shape, in_specs, out_specs, scratch, vmem_mib=16, **options):
        return pl.pallas_call(
            kernel,
            out_shape=out_shape,
            in_specs=in_specs,
            out_specs=out_specs,
            scratch_shapes=scratch,
            compiler_params=pltpu.CompilerParams(vmem_limit_bytes=vmem_mib * MIB),
            cost_estimate=COST,
            **options,
        )

    def own_chunks(*ks, until=(), space=ANY, vmem_mib=16):
        return call(
            functools.partial(chunk_kernel, ks),
            [chunk(k) for k in ks],
            [ANY] * (1 + len(until)),
            [space] * len(ks),
            [pltpu.SemaphoreType.DMA((len(ks),))],
            vmem_mib,
        )(queries, *until)

    def step(k, *until):
        out = call(
            functools.partial(step_kernel, k),
            chunk(k),
            [ANY] * (2 + len(until)),
            ANY,
            [pltpu.SemaphoreType.DMA],
        )(queries, far[k], *until)
        near[k] = lax.ppermute(out, "dp", pair)
        return out

    def send_ahead(k, *until):
        (sent,) = own_chunks(k, until=until)
        far[k] = lax.ppermute(sent, "dp", ahead)
        return sent

    def pair_scores(*ks, sums=None, until=()):
        operands = [*held, inverse] + [block[k] for k in ks for block in (near, far)]
        if sums is not None:
            operands.append(sums)
        return call(
            functools.partial(pair_kernel, ks, sums is None),
            floats(doc_rows, 2 * rows),
            [VMEM] * len(operands) + [ANY] * len(until),
            VMEM,
            [pltpu.VMEM((2 * rows, max(width_of(k, dims) for k in ks)), queries.dtype)],
        )(*operands, *until)

    def send_across(block, k, *until):
        sent = lax.optimization_barrier((block[k], *until))[0]
        block[CHUNKS - 1 - k] = lax.ppermute(sent, "groups", across)

    far = [None] * CHUNKS
    near = [None] * CHUNKS

    sent = own_chunks(0, 1, space=VMEM, vmem_mib=59)
    for k in range(2):
        far[k] = lax.ppermute(sent[k], "dp", ahead)

    def own_scores(part, *operands, until=()):
        pieces = 4
        outs = [
            floats(doc_rows, rows),
            jax.ShapeDtypeStruct((doc_rows, dims // 2), documents.dtype),
            floats(1, dims),
        ][: 3 - part]
        return call(
            functools.partial(own_kernel, part, pieces),
            outs,
            [HBM] + [VMEM] * (1 + len(operands)) + [ANY] * len(until),
            [VMEM] * len(outs),
            [pltpu.SemaphoreType.DMA((pieces, 2))],
            vmem_mib=OWN_MIB[part],
        )(documents, queries, *operands, *until)

    kept = lax.optimization_barrier((eigenvalues, sent[1]))[0].reshape(1, dims)
    own_sums, held0, inverse = own_scores(0, kept)

    out = step(0, inverse)
    out = send_ahead(2, out)
    send_across(far, 0, out)
    own_sums, held1 = own_scores(1, inverse, own_sums, until=(out,))
    held = held0, held1

    out = step(1, own_sums)
    out = send_ahead(3, out)
    send_across(near, 0, out)
    sums = pair_scores(0, until=(out, far[5]))

    out = step(2, sums)
    out = send_ahead(4, out)
    send_across(near, 1, out)
    sums = pair_scores(1, sums=sums, until=(out,))

    out = step(3, sums)
    sums = pair_scores(2, 5, sums=sums, until=(out,))

    operands = [counts, *held, inverse, near[4], far[4], far[3], sums, own_sums]
    near_sums, theirs, mine = call(
        functools.partial(far_kernel, (4,), 3, factor),
        [floats(doc_rows, rows), floats(half, 2 * rows), floats(half, 2 * rows)],
        [SMEM] + [VMEM] * (len(operands) - 1),
        [VMEM] * 3,
        [
            pltpu.VMEM((doc_rows, 2 * rows), jnp.float32),
            pltpu.VMEM((2 * rows, width_of(4, dims)), queries.dtype),
        ],
    )(*operands)
    got = lax.ppermute(theirs, "layer", across)

    def near_scores(side, until):
        return call(
            functools.partial(near_kernel, 3, side, factor),
            floats(half, rows),
            [SMEM] + [VMEM] * 5 + [ANY],
            VMEM,
            [],
        )(counts, *held, inverse, near[3], near_sums, until)

    theirs_near = near_scores(0, theirs)
    got_near = lax.ppermute(theirs_near, "layer", across)
    mine_near = near_scores(1, theirs_near)
    return call(final_kernel, floats(half, 3 * rows), [VMEM] * 4, VMEM, [])(
        mine, got, mine_near, got_near
    )


def solution(mesh):
    return jax.shard_map(
        on_device,
        mesh=mesh,
        in_specs=(P("dp", "layer"), P(("groups", "dp"), "layer"), P(("groups", "dp")), P("layer")),
        out_specs=P(("groups", "dp", "layer"), None),
        check_vma=False,
    )
```

```python
import functools
import math

import jax
import jax.numpy as jnp
from jax import lax
from jax.experimental import pallas as pl
from jax.experimental.pallas import tpu as pltpu
from jax.sharding import PartitionSpec as P

L_DIM = 8192
SIZES = (12, 12, 8, 8, 12, 12)
CHUNKS = len(SIZES)
DIRECT = 5
OWN_MIB = (44, 40)
VMEM = pl.BlockSpec(memory_space=pltpu.VMEM)
SMEM = pl.BlockSpec(memory_space=pltpu.SMEM)
HBM = pl.BlockSpec(memory_space=pltpu.HBM)
ANY = pl.BlockSpec(memory_space=pl.ANY)
COST = pl.CostEstimate(flops=16 * 10**8, bytes_accessed=0, transcendentals=0)
MIB = 1024 * 1024


def width_of(k, dims):
    return SIZES[k] * dims // sum(SIZES)


def columns_of(k, dims, within=None):
    unit = dims // sum(SIZES)
    left, right = sum(SIZES[:k]), sum(SIZES[k + 1 :])
    if within:
        left, right = left % (sum(SIZES) // 2), right % (sum(SIZES) // 2)
    start = jnp.where(lax.axis_index("groups") == 0, left * unit, right * unit)
    return pl.ds(pl.multiple_of(start, unit), width_of(k, dims))


def half_columns(part, dims):
    group = lax.axis_index("groups")
    side = group if part == 0 else 1 - group
    return pl.ds(pl.multiple_of(side * (dims // 2), dims // 2), dims // 2)


def products(rows, block):
    return lax.dot_general(
        rows, block, (((1,), (1,)), ((), ())), preferred_element_type=jnp.float32
    )


def scale_of(factor, counts, half, side):
    layer = lax.axis_index("layer")
    start = (layer if side else 1 - layer) * half
    index = start + lax.broadcasted_iota(jnp.int32, (half, 1), 0)
    return factor * (index < counts[0]).astype(jnp.float32)


def chunk_kernel(ks, queries, *refs):
    outs, sem = refs[-len(ks) - 1 : -1], refs[-1]
    dims = queries.shape[1]
    copies = [
        pltpu.make_async_copy(queries.at[:, columns_of(k, dims)], outs[i], sem.at[i])
        for i, k in enumerate(ks)
    ]
    for copy in copies:
        copy.start()
    for copy in copies:
        copy.wait()


def step_kernel(k, queries, received, *refs):
    out, sem = refs[-2:]
    even = lax.axis_index("dp") % 2 == 0
    own_copy = pltpu.make_async_copy(queries.at[:, columns_of(k, queries.shape[1])], out, sem)
    received_copy = pltpu.make_async_copy(received, out, sem)

    @pl.when(even)
    def _():
        own_copy.start()
        own_copy.wait()

    @pl.when(jnp.logical_not(even))
    def _():
        received_copy.start()
        received_copy.wait()


def own_kernel(part, pieces, factor, counts, documents, queries, *refs):
    if part == 0:
        eigenvalues, theirs, mine, held, inverse, sem = refs[0], *refs[-5:]
        before = None
    else:
        inverse, before, theirs, mine, held, sem = refs[0], refs[1:3], *refs[-4:]
    layer = lax.axis_index("layer")
    half = documents.shape[0] // 2
    dims = documents.shape[1]
    width = dims // 2 // pieces
    first = half_columns(part, dims).start
    copies = []
    for i in range(pieces):
        start = pl.multiple_of(first + i * width, width)
        for at, row in enumerate((1 - layer, layer)):
            copies.append(
                pltpu.make_async_copy(
                    documents.at[pl.ds(pl.multiple_of(row * half, half), half), pl.ds(start, width)],
                    held.at[pl.ds(at * half, half), pl.ds(i * width, width)],
                    sem.at[i, at],
                )
            )
    for copy in copies:
        copy.start()
    if part == 0:
        for start in range(0, dims, L_DIM):
            block = eigenvalues[:, start : start + L_DIM]
            damping = 0.1 * jnp.mean(block, axis=1, keepdims=True)
            inverse[:, start : start + L_DIM] = 1.0 / (block + damping)
    for i in range(pieces):
        columns = pl.ds(pl.multiple_of(first + i * width, width), width)
        scaled = (queries[:, columns].astype(jnp.float32) * inverse[:, columns]).astype(jnp.bfloat16)
        for side, out in enumerate((theirs, mine)):
            copies[2 * i + side].wait()
            term = products(
                held[side * half : (side + 1) * half, i * width : (i + 1) * width], scaled
            )
            if i > 0:
                out[...] += term
            elif part == 0:
                out[...] = term
            else:
                out[...] = before[side][...] + term
    if part == 1:
        theirs[...] *= scale_of(factor, counts, half, 0)
        mine[...] *= scale_of(factor, counts, half, 1)


def held_of(k, held):
    return held[0] if k < CHUNKS // 2 else held[1]


def pair_kernel(ks, side, factor, fresh, counts, held0, held1, inverse, *refs):
    count = len(ks)
    chunks, out, block_buf = refs[: 2 * count], refs[-2], refs[-1]
    dims = inverse.shape[1]
    size = out.shape[0]
    first = 0 if side is None else side * size
    rows = chunks[0].shape[0]
    for i, k in enumerate(ks):
        width = width_of(k, dims)
        for b in range(2):
            scaled = chunks[2 * i + b][...].astype(jnp.float32) * inverse[:, columns_of(k, dims)]
            block_buf[pl.ds(b * rows, rows), :width] = scaled.astype(jnp.bfloat16)
        held = held_of(k, (held0, held1))
        term = products(held[first : first + size, columns_of(k, dims, True)], block_buf[:, :width])
        if i > 0:
            out[...] += term
        elif fresh:
            out[...] = term
        else:
            out[...] = refs[2 * count][first : first + size] + term
    if side is not None:
        out[...] *= scale_of(factor, counts, size, side)


def final_kernel(mine0, got0, mine, got, out):
    rows = mine0.shape[1]
    out[:, :rows] = mine0[...] + got0[...]
    out[:, rows:] = mine[...] + got[...]


def on_device(queries, documents, counts, eigenvalues):
    rows, dims = queries.shape
    doc_rows = documents.shape[0]
    half = doc_rows // 2
    owners = lax.axis_size("dp")
    factor = 1.0 / math.sqrt(dims * lax.axis_size("layer"))
    ahead = [(i, (i + 2) % owners) for i in range(owners)]
    pair = [(i, i ^ 1) for i in range(owners)]
    across = [(0, 1), (1, 0)]

    def chunk(k):
        return jax.ShapeDtypeStruct((rows, width_of(k, dims)), queries.dtype)

    def floats(*shape):
        return jax.ShapeDtypeStruct(shape, jnp.float32)

    def call(kernel, out_shape, in_specs, out_specs, scratch, vmem_mib=16, **options):
        return pl.pallas_call(
            kernel,
            out_shape=out_shape,
            in_specs=in_specs,
            out_specs=out_specs,
            scratch_shapes=scratch,
            compiler_params=pltpu.CompilerParams(vmem_limit_bytes=vmem_mib * MIB),
            cost_estimate=COST,
            **options,
        )

    def own_chunks(*ks, until=(), space=ANY, vmem_mib=16):
        return call(
            functools.partial(chunk_kernel, ks),
            [chunk(k) for k in ks],
            [ANY] * (1 + len(until)),
            [space] * len(ks),
            [pltpu.SemaphoreType.DMA((len(ks),))],
            vmem_mib,
        )(queries, *until)

    def step(k, *until):
        out = call(
            functools.partial(step_kernel, k),
            chunk(k),
            [ANY] * (2 + len(until)),
            ANY,
            [pltpu.SemaphoreType.DMA],
        )(queries, far[k], *until)
        near[k] = lax.ppermute(out, "dp", pair)
        return out

    def send_ahead(k, *until):
        (sent,) = own_chunks(k, until=until)
        far[k] = lax.ppermute(sent, "dp", ahead)
        return sent

    def pair_scores(*ks, sums=None, side=None, until=()):
        operands = [*held, inverse] + [block[k] for k in ks for block in (near, far)]
        if sums is not None:
            operands.append(sums)
        return call(
            functools.partial(pair_kernel, ks, side, factor, sums is None),
            floats(doc_rows if side is None else half, 2 * rows),
            [SMEM] + [VMEM] * len(operands) + [ANY] * len(until),
            VMEM,
            [pltpu.VMEM((2 * rows, max(width_of(k, dims) for k in ks)), queries.dtype)],
        )(counts, *operands, *until)

    def send_across(block, k, *until):
        sent = lax.optimization_barrier((block[k], *until))[0]
        block[CHUNKS - 1 - k] = lax.ppermute(sent, "groups", across)

    far = [None] * CHUNKS
    near = [None] * CHUNKS

    sent = own_chunks(0, 1, space=VMEM, vmem_mib=53)
    for k in range(2):
        far[k] = lax.ppermute(sent[k], "dp", ahead)

    def own_scores(part, *operands, until=()):
        pieces = 4
        outs = [
            floats(half, rows),
            floats(half, rows),
            jax.ShapeDtypeStruct((doc_rows, dims // 2), documents.dtype),
            floats(1, dims),
        ][: 4 - part]
        return call(
            functools.partial(own_kernel, part, pieces, factor),
            outs,
            [SMEM, HBM] + [VMEM] * (1 + len(operands)) + [ANY] * len(until),
            [VMEM] * len(outs),
            [pltpu.SemaphoreType.DMA((pieces, 2))],
            vmem_mib=OWN_MIB[part],
        )(counts, documents, queries, *operands, *until)

    kept = lax.optimization_barrier((eigenvalues, sent[1]))[0].reshape(1, dims)
    theirs0, mine0, held0, inverse = own_scores(0, kept)

    out = step(0, inverse)
    out = send_ahead(2, out)
    send_across(far, 0, out)
    theirs0, mine0, held1 = own_scores(1, inverse, theirs0, mine0, until=(out,))
    held = held0, held1

    out = step(1, theirs0)
    out = send_ahead(3, out)
    send_across(near, 0, out)
    sums = pair_scores(0, until=(out, far[5]))

    out = step(2, sums)
    out = send_ahead(4, out)
    send_across(near, 1, out)
    sums = pair_scores(1, sums=sums, until=(out,))

    out = step(3, sums)
    got0 = lax.ppermute(lax.optimization_barrier((theirs0, out))[0], "layer", across)
    sums = pair_scores(2, 5, sums=sums, until=(out,))
    theirs = pair_scores(3, 4, sums=sums, side=0, until=(got0,))
    got = lax.ppermute(theirs, "layer", across)
    mine = pair_scores(3, 4, sums=sums, side=1, until=(theirs,))
    return call(final_kernel, floats(half, 3 * rows), [VMEM] * 4, VMEM, [])(mine0, got0, mine, got)


def solution(mesh):
    return jax.shard_map(
        on_device,
        mesh=mesh,
        in_specs=(P("dp", "layer"), P(("groups", "dp"), "layer"), P(("groups", "dp")), P("layer")),
        out_specs=P(("groups", "dp", "layer"), None),
        check_vma=False,
    )
```

```python
import functools
import math

import jax
import jax.numpy as jnp
from jax import lax
from jax.experimental import pallas as pl
from jax.experimental.pallas import tpu as pltpu
from jax.sharding import PartitionSpec as P

L_DIM = 8192
SIZES = (11, 13, 8, 8, 13, 11)
CHUNKS = len(SIZES)
DIRECT = 5
PARTS = 4
OWN_MIB = (44, 40)
VMEM = pl.BlockSpec(memory_space=pltpu.VMEM)
SMEM = pl.BlockSpec(memory_space=pltpu.SMEM)
HBM = pl.BlockSpec(memory_space=pltpu.HBM)
ANY = pl.BlockSpec(memory_space=pl.ANY)
COST = pl.CostEstimate(flops=18*10**8, bytes_accessed=0, transcendentals=0)
MIB = 1024 * 1024


def width_of(k, dims):
    return SIZES[k] * dims // sum(SIZES)


def columns_of(k, dims, within=None):
    unit = dims // sum(SIZES)
    left, right = sum(SIZES[:k]), sum(SIZES[k + 1 :])
    if within:
        left, right = left % (sum(SIZES) // 2), right % (sum(SIZES) // 2)
    start = jnp.where(lax.axis_index("groups") == 0, left * unit, right * unit)
    return pl.ds(pl.multiple_of(start, unit), width_of(k, dims))


def half_columns(part, dims):
    group = lax.axis_index("groups")
    side = group if part == 0 else 1 - group
    return pl.ds(pl.multiple_of(side * (dims // 2), dims // 2), dims // 2)


def products(rows, block):
    return lax.dot_general(
        rows, block, (((1,), (1,)), ((), ())), preferred_element_type=jnp.float32
    )


def scale_of(factor, counts, half, side):
    layer = lax.axis_index("layer")
    start = (layer if side else 1 - layer) * half
    index = start + lax.broadcasted_iota(jnp.int32, (half, 1), 0)
    return factor * (index < counts[0]).astype(jnp.float32)


def row_parts(rows, parts):
    size = rows // parts
    return [pl.ds(i * size, size) for i in range(parts)]


def chunk_kernel(ks, queries, *refs):
    outs, sem = refs[-len(ks) - 1 : -1], refs[-1]
    rows, dims = queries.shape
    copies = [
        pltpu.make_async_copy(
            queries.at[part, columns_of(k, dims)], outs[i].at[part], sem.at[i, p]
        )
        for i, k in enumerate(ks)
        for p, part in enumerate(row_parts(rows, PARTS))
    ]
    for copy in copies:
        copy.start()
    for copy in copies:
        copy.wait()


def step_kernel(k, queries, received, *refs):
    out, sem = refs[-2:]
    even = lax.axis_index("dp") % 2 == 0
    own_copy = pltpu.make_async_copy(queries.at[:, columns_of(k, queries.shape[1])], out, sem)
    received_copy = pltpu.make_async_copy(received, out, sem)

    @pl.when(even)
    def _():
        own_copy.start()
        own_copy.wait()

    @pl.when(jnp.logical_not(even))
    def _():
        received_copy.start()
        received_copy.wait()


def own_kernel(part, pieces, factor, counts, documents, queries, *refs):
    if part == 0:
        eigenvalues, theirs, mine, held, inverse, sem = refs[0], *refs[-5:]
        before = None
    else:
        inverse, before, theirs, mine, held, sem = refs[0], refs[1:3], *refs[-4:]
    layer = lax.axis_index("layer")
    half = documents.shape[0] // 2
    dims = documents.shape[1]
    width = dims // 2 // pieces
    first = half_columns(part, dims).start
    size = half // PARTS
    copies = {}
    for i in range(pieces):
        start = pl.multiple_of(first + i * width, width)
        for side, row in enumerate((1 - layer, layer)):
            copies[i, side] = [
                pltpu.make_async_copy(
                    documents.at[
                        pl.ds(pl.multiple_of(row * half + p * size, size), size),
                        pl.ds(start, width),
                    ],
                    held.at[pl.ds(side * half + p * size, size), pl.ds(i * width, width)],
                    sem.at[i, side, p],
                )
                for p in range(PARTS)
            ]
            for copy in copies[i, side]:
                copy.start()
    if part == 0:
        for start in range(0, dims, L_DIM):
            block = eigenvalues[:, start : start + L_DIM]
            damping = 0.1 * jnp.mean(block, axis=1, keepdims=True)
            inverse[:, start : start + L_DIM] = 1.0 / (block + damping)
    for i in range(pieces):
        columns = pl.ds(pl.multiple_of(first + i * width, width), width)
        scaled = (queries[:, columns].astype(jnp.float32) * inverse[:, columns]).astype(jnp.bfloat16)
        for side, out in enumerate((theirs, mine)):
            for copy in copies[i, side]:
                copy.wait()
            term = products(
                held[side * half : (side + 1) * half, i * width : (i + 1) * width], scaled
            )
            if i > 0:
                out[...] += term
            elif part == 0:
                out[...] = term
            else:
                out[...] = before[side][...] + term
    if part == 1:
        theirs[...] *= scale_of(factor, counts, half, 0)
        mine[...] *= scale_of(factor, counts, half, 1)


def held_of(k, held):
    return held[0] if k < CHUNKS // 2 else held[1]


def pair_kernel(ks, side, factor, fresh, counts, held0, held1, inverse, *refs):
    count = len(ks)
    chunks, out, block_buf = refs[: 2 * count], refs[-2], refs[-1]
    dims = inverse.shape[1]
    size = out.shape[0]
    first = 0 if side is None else side * size
    rows = chunks[0].shape[0]
    for i, k in enumerate(ks):
        width = width_of(k, dims)
        for b in range(2):
            scaled = chunks[2 * i + b][...].astype(jnp.float32) * inverse[:, columns_of(k, dims)]
            block_buf[pl.ds(b * rows, rows), :width] = scaled.astype(jnp.bfloat16)
        held = held_of(k, (held0, held1))
        term = products(held[first : first + size, columns_of(k, dims, True)], block_buf[:, :width])
        if i > 0:
            out[...] += term
        elif fresh:
            out[...] = term
        else:
            out[...] = refs[2 * count][first : first + size] + term
    if side is not None:
        out[...] *= scale_of(factor, counts, size, side)


def final_kernel(mine0, got0, mine, got, out, buf, sem):
    half, rows = mine0.shape
    copies = []
    for p, part in enumerate(row_parts(half, PARTS)):
        buf[part, :rows] = mine0[part, :] + got0[part, :]
        buf[part, rows:] = mine[part, :] + got[part, :]
        copies.append(pltpu.make_async_copy(buf.at[part], out.at[part], sem.at[p]))
        copies[p].start()
    for copy in copies:
        copy.wait()


def on_device(queries, documents, counts, eigenvalues):
    rows, dims = queries.shape
    doc_rows = documents.shape[0]
    half = doc_rows // 2
    owners = lax.axis_size("dp")
    factor = 1.0 / math.sqrt(dims * lax.axis_size("layer"))
    ahead = [(i, (i + 2) % owners) for i in range(owners)]
    pair = [(i, i ^ 1) for i in range(owners)]
    across = [(0, 1), (1, 0)]

    def chunk(k):
        return jax.ShapeDtypeStruct((rows, width_of(k, dims)), queries.dtype)

    def floats(*shape):
        return jax.ShapeDtypeStruct(shape, jnp.float32)

    def call(kernel, out_shape, in_specs, out_specs, scratch, vmem_mib=16, **options):
        return pl.pallas_call(
            kernel,
            out_shape=out_shape,
            in_specs=in_specs,
            out_specs=out_specs,
            scratch_shapes=scratch,
            compiler_params=pltpu.CompilerParams(vmem_limit_bytes=vmem_mib * MIB),
            cost_estimate=COST,
            **options,
        )

    def own_chunks(*ks, until=(), space=ANY, vmem_mib=16):
        return call(
            functools.partial(chunk_kernel, ks),
            [chunk(k) for k in ks],
            [ANY] * (1 + len(until)),
            [space] * len(ks),
            [pltpu.SemaphoreType.DMA((len(ks), PARTS))],
            vmem_mib,
        )(queries, *until)

    def step(k, *until):
        out = call(
            functools.partial(step_kernel, k),
            chunk(k),
            [ANY] * (2 + len(until)),
            ANY,
            [pltpu.SemaphoreType.DMA],
        )(queries, far[k], *until)
        near[k] = lax.ppermute(out, "dp", pair)
        return out

    def send_ahead(k, *until):
        (sent,) = own_chunks(k, until=until)
        far[k] = lax.ppermute(sent, "dp", ahead)
        return sent

    def pair_scores(*ks, sums=None, side=None, until=()):
        operands = [*held, inverse] + [block[k] for k in ks for block in (near, far)]
        if sums is not None:
            operands.append(sums)
        return call(
            functools.partial(pair_kernel, ks, side, factor, sums is None),
            floats(doc_rows if side is None else half, 2 * rows),
            [SMEM] + [VMEM] * len(operands) + [ANY] * len(until),
            VMEM,
            [pltpu.VMEM((2 * rows, max(width_of(k, dims) for k in ks)), queries.dtype)],
        )(counts, *operands, *until)

    def send_across(block, k, *until):
        sent = lax.optimization_barrier((block[k], *until))[0]
        block[CHUNKS - 1 - k] = lax.ppermute(sent, "groups", across)

    far = [None] * CHUNKS
    near = [None] * CHUNKS

    sent = own_chunks(0, 1, space=VMEM, vmem_mib=53)
    for k in range(2):
        far[k] = lax.ppermute(sent[k], "dp", ahead)

    def own_scores(part, *operands, until=()):
        pieces = 4
        outs = [
            floats(half, rows),
            floats(half, rows),
            jax.ShapeDtypeStruct((doc_rows, dims // 2), documents.dtype),
            floats(1, dims),
        ][: 4 - part]
        return call(
            functools.partial(own_kernel, part, pieces, factor),
            outs,
            [SMEM, HBM] + [VMEM] * (1 + len(operands)) + [ANY] * len(until),
            [VMEM] * len(outs),
            [pltpu.SemaphoreType.DMA((pieces, 2, PARTS))],
            vmem_mib=OWN_MIB[part],
        )(counts, documents, queries, *operands, *until)

    kept = lax.optimization_barrier((eigenvalues, sent[1]))[0].reshape(1, dims)
    theirs0, mine0, held0, inverse = own_scores(0, kept)

    out = step(0, inverse)
    out = send_ahead(2, out)
    send_across(far, 0, out)
    theirs0, mine0, held1 = own_scores(1, inverse, theirs0, mine0, until=(out,))
    held = held0, held1

    out = step(1, theirs0)
    out = send_ahead(3, out)
    send_across(near, 0, out)
    sums = pair_scores(0, until=(out, far[5]))

    out = step(2, sums)
    out = send_ahead(4, out)
    send_across(near, 1, out)
    sums = pair_scores(1, sums=sums, until=(out,))

    out = step(3, sums)
    got0 = lax.ppermute(lax.optimization_barrier((theirs0, out))[0], "layer", across)
    sums = pair_scores(2, 5, sums=sums, until=(out,))
    sums = pair_scores(4, sums=sums, until=(got0,))
    theirs = pair_scores(3, sums=sums, side=0)
    got = lax.ppermute(theirs, "layer", across)
    mine = pair_scores(3, sums=sums, side=1, until=(theirs,))
    return call(
        final_kernel,
        floats(half, 3 * rows),
        [VMEM] * 4,
        HBM,
        [pltpu.VMEM((half, 3 * rows), jnp.float32), pltpu.SemaphoreType.DMA((PARTS,))],
    )(mine0, got0, mine, got)


def solution(mesh):
    return jax.shard_map(
        on_device,
        mesh=mesh,
        in_specs=(P("dp", "layer"), P(("groups", "dp"), "layer"), P(("groups", "dp")), P("layer")),
        out_specs=P(("groups", "dp", "layer"), None),
        check_vma=False,
    )
```

```python
import functools
import math

import jax
import jax.numpy as jnp
from jax import lax
from jax.experimental import pallas as pl
from jax.experimental.pallas import tpu as pltpu
from jax.sharding import PartitionSpec as P

L_DIM = 8192
SIZES = (12, 12, 8, 8, 12, 12)
CHUNKS = len(SIZES)
DIRECT = 5
OWN_MIB = (44, 40)
TILE = 4
VMEM = pl.BlockSpec(memory_space=pltpu.VMEM)
SMEM = pl.BlockSpec(memory_space=pltpu.SMEM)
HBM = pl.BlockSpec(memory_space=pltpu.HBM)
ANY = pl.BlockSpec(memory_space=pl.ANY)
COST = pl.CostEstimate(flops=16*10**8, bytes_accessed=0, transcendentals=0)
MIB = 1024 * 1024


def width_of(k, dims):
    return SIZES[k] * dims // sum(SIZES)


def columns_of(k, dims, within=None):
    unit = dims // sum(SIZES)
    left, right = sum(SIZES[:k]), sum(SIZES[k + 1 :])
    if within:
        left, right = left % (sum(SIZES) // 2), right % (sum(SIZES) // 2)
    start = jnp.where(lax.axis_index("groups") == 0, left * unit, right * unit)
    return pl.ds(pl.multiple_of(start, unit), width_of(k, dims))


def half_columns(part, dims):
    group = lax.axis_index("groups")
    side = group if part == 0 else 1 - group
    return pl.ds(pl.multiple_of(side * (dims // 2), dims // 2), dims // 2)


def products(rows, block):
    return lax.dot_general(
        rows, block, (((1,), (1,)), ((), ())), preferred_element_type=jnp.float32
    )


def scale_of(factor, counts, half, side):
    layer = lax.axis_index("layer")
    start = (layer if side else 1 - layer) * half
    index = start + lax.broadcasted_iota(jnp.int32, (half, 1), 0)
    return factor * (index < counts[0]).astype(jnp.float32)


def chunk_kernel(ks, queries, *refs):
    outs, sem = refs[-len(ks) - 1 : -1], refs[-1]
    dims = queries.shape[1]
    copies = [
        pltpu.make_async_copy(queries.at[:, columns_of(k, dims)], outs[i], sem.at[i])
        for i, k in enumerate(ks)
    ]
    for copy in copies:
        copy.start()
    for copy in copies:
        copy.wait()


def step_kernel(k, queries, received, *refs):
    out, sem = refs[-2:]
    even = lax.axis_index("dp") % 2 == 0
    own_copy = pltpu.make_async_copy(queries.at[:, columns_of(k, queries.shape[1])], out, sem)
    received_copy = pltpu.make_async_copy(received, out, sem)

    @pl.when(even)
    def _():
        own_copy.start()
        own_copy.wait()

    @pl.when(jnp.logical_not(even))
    def _():
        received_copy.start()
        received_copy.wait()


def tile_of(dims):
    return TILE * dims // sum(SIZES)


def own_kernel(part, factor, counts, documents, queries, *refs):
    if part == 0:
        eigenvalues, sums, held, inverse, sem = refs[0], *refs[-4:]
    else:
        inverse, before, theirs, mine, held, sums, sem = refs[0], refs[1], *refs[-5:]
    layer = lax.axis_index("layer")
    half = documents.shape[0] // 2
    dims = documents.shape[1]
    tile = tile_of(dims)
    first = half_columns(part, dims).start

    def copies(i):
        start = pl.multiple_of(first + i * tile, tile)
        return [
            pltpu.make_async_copy(
                documents.at[pl.ds(pl.multiple_of(row * half, half), half), pl.ds(start, tile)],
                held.at[pl.ds(side * half, half), pl.ds(pl.multiple_of(i * tile, tile), tile)],
                sem.at[i, side],
            )
            for side, row in enumerate((1 - layer, layer))
        ]

    @pl.loop(0, dims // 2 // tile)
    def _(i):
        for copy in copies(i):
            copy.start()

    if part == 0:
        for start in range(0, dims, L_DIM):
            block = eigenvalues[:, start : start + L_DIM]
            damping = 0.1 * jnp.mean(block, axis=1, keepdims=True)
            inverse[:, start : start + L_DIM] = 1.0 / (block + damping)
        sums[...] = jnp.zeros_like(sums)
    else:
        sums[...] = before[...]

    @pl.loop(0, dims // 2 // tile)
    def _(i):
        columns = pl.ds(pl.multiple_of(first + i * tile, tile), tile)
        scaled = (queries[:, columns].astype(jnp.float32) * inverse[:, columns]).astype(jnp.bfloat16)
        for copy in copies(i):
            copy.wait()
        sums[...] += products(held[:, pl.ds(pl.multiple_of(i * tile, tile), tile)], scaled)

    if part == 1:
        theirs[...] = sums[:half] * scale_of(factor, counts, half, 0)
        mine[...] = sums[half:] * scale_of(factor, counts, half, 1)


def held_of(k, held):
    return held[0] if k < CHUNKS // 2 else held[1]


def pair_kernel(ks, side, factor, fresh, counts, held0, held1, inverse, *refs):
    chunks, out, block = refs[: 2 * len(ks)], refs[-2], refs[-1]
    dims = inverse.shape[1]
    tile = tile_of(dims)
    size = out.shape[0]
    first = 0 if side is None else side * size
    rows = chunks[0].shape[0]
    out[...] = jnp.zeros_like(out) if fresh else refs[2 * len(ks)][first : first + size]
    for i, k in enumerate(ks):
        held = held_of(k, (held0, held1))
        at, held_at = columns_of(k, dims).start, columns_of(k, dims, True).start

        @pl.loop(0, width_of(k, dims) // tile)
        def _(t, i=i, held=held, at=at, held_at=held_at):
            shift = t * tile
            scale = inverse[:, pl.ds(pl.multiple_of(at + shift, tile), tile)]
            for b in range(2):
                chunk = chunks[2 * i + b][:, pl.ds(pl.multiple_of(shift, tile), tile)]
                block[b * rows : (b + 1) * rows, :] = (chunk.astype(jnp.float32) * scale).astype(
                    jnp.bfloat16
                )
            columns = pl.ds(pl.multiple_of(held_at + shift, tile), tile)
            out[...] += products(held[first : first + size, columns], block[...])

    if side is not None:
        out[...] *= scale_of(factor, counts, size, side)


def final_kernel(mine0, got0, mine, got, out):
    rows = mine0.shape[1]
    out[:, :rows] = mine0[...] + got0[...]
    out[:, rows:] = mine[...] + got[...]


def on_device(queries, documents, counts, eigenvalues):
    rows, dims = queries.shape
    doc_rows = documents.shape[0]
    half = doc_rows // 2
    owners = lax.axis_size("dp")
    factor = 1.0 / math.sqrt(dims * lax.axis_size("layer"))
    ahead = [(i, (i + 2) % owners) for i in range(owners)]
    pair = [(i, i ^ 1) for i in range(owners)]
    across = [(0, 1), (1, 0)]

    def chunk(k):
        return jax.ShapeDtypeStruct((rows, width_of(k, dims)), queries.dtype)

    def floats(*shape):
        return jax.ShapeDtypeStruct(shape, jnp.float32)

    def call(kernel, out_shape, in_specs, out_specs, scratch, vmem_mib=16, **options):
        return pl.pallas_call(
            kernel,
            out_shape=out_shape,
            in_specs=in_specs,
            out_specs=out_specs,
            scratch_shapes=scratch,
            compiler_params=pltpu.CompilerParams(vmem_limit_bytes=vmem_mib * MIB),
            cost_estimate=COST,
            **options,
        )

    def own_chunks(*ks, until=(), space=ANY, vmem_mib=16):
        return call(
            functools.partial(chunk_kernel, ks),
            [chunk(k) for k in ks],
            [ANY] * (1 + len(until)),
            [space] * len(ks),
            [pltpu.SemaphoreType.DMA((len(ks),))],
            vmem_mib,
        )(queries, *until)

    def step(k, *until):
        out = call(
            functools.partial(step_kernel, k),
            chunk(k),
            [ANY] * (2 + len(until)),
            ANY,
            [pltpu.SemaphoreType.DMA],
        )(queries, far[k], *until)
        near[k] = lax.ppermute(out, "dp", pair)
        return out

    def send_ahead(k, *until):
        (sent,) = own_chunks(k, until=until)
        far[k] = lax.ppermute(sent, "dp", ahead)
        return sent

    def pair_scores(*ks, sums=None, side=None, until=()):
        operands = [*held, inverse] + [block[k] for k in ks for block in (near, far)]
        if sums is not None:
            operands.append(sums)
        return call(
            functools.partial(pair_kernel, ks, side, factor, sums is None),
            floats(doc_rows if side is None else half, 2 * rows),
            [SMEM] + [VMEM] * len(operands) + [ANY] * len(until),
            VMEM,
            [pltpu.VMEM((2 * rows, tile_of(dims)), queries.dtype)],
        )(counts, *operands, *until)

    def send_across(block, k, *until):
        sent = lax.optimization_barrier((block[k], *until))[0]
        block[CHUNKS - 1 - k] = lax.ppermute(sent, "groups", across)

    far = [None] * CHUNKS
    near = [None] * CHUNKS

    sent = own_chunks(0, 1, space=VMEM, vmem_mib=53)
    for k in range(2):
        far[k] = lax.ppermute(sent[k], "dp", ahead)

    def own_scores(part, *operands, until=()):
        sums = floats(doc_rows, rows)
        keep = jax.ShapeDtypeStruct((doc_rows, dims // 2), documents.dtype)
        semaphores = pltpu.SemaphoreType.DMA((dims // 2 // tile_of(dims), 2))
        if part == 0:
            outs, scratch = [sums, keep, floats(1, dims)], [semaphores]
        else:
            outs = [floats(half, rows), floats(half, rows), keep]
            scratch = [pltpu.VMEM(sums.shape, sums.dtype), semaphores]
        return call(
            functools.partial(own_kernel, part, factor),
            outs,
            [SMEM, HBM] + [VMEM] * (1 + len(operands)) + [ANY] * len(until),
            [VMEM] * 3,
            scratch,
            vmem_mib=OWN_MIB[part],
        )(counts, documents, queries, *operands, *until)

    kept = lax.optimization_barrier((eigenvalues, sent[1]))[0].reshape(1, dims)
    own_sums, held0, inverse = own_scores(0, kept)

    out = step(0, inverse)
    out = send_ahead(2, out)
    send_across(far, 0, out)
    theirs0, mine0, held1 = own_scores(1, inverse, own_sums, until=(out,))
    held = held0, held1

    out = step(1, theirs0)
    out = send_ahead(3, out)
    send_across(near, 0, out)
    sums = pair_scores(0, until=(out, far[5]))

    out = step(2, sums)
    out = send_ahead(4, out)
    send_across(near, 1, out)
    sums = pair_scores(1, sums=sums, until=(out,))

    out = step(3, sums)
    got0 = lax.ppermute(lax.optimization_barrier((theirs0, out))[0], "layer", across)
    sums = pair_scores(2, 5, sums=sums, until=(out,))
    theirs = pair_scores(3, 4, sums=sums, side=0, until=(got0,))
    got = lax.ppermute(theirs, "layer", across)
    mine = pair_scores(3, 4, sums=sums, side=1, until=(theirs,))
    return call(final_kernel, floats(half, 3 * rows), [VMEM] * 4, VMEM, [])(mine0, got0, mine, got)


def solution(mesh):
    return jax.shard_map(
        on_device,
        mesh=mesh,
        in_specs=(P("dp", "layer"), P(("groups", "dp"), "layer"), P(("groups", "dp")), P("layer")),
        out_specs=P(("groups", "dp", "layer"), None),
        check_vma=False,
    )
```

```python
import functools
import math

import jax
import jax.numpy as jnp
from jax import lax
from jax.experimental import pallas as pl
from jax.experimental.pallas import tpu as pltpu
from jax.sharding import PartitionSpec as P

L_DIM = 8192
SIZES = (8, 8, 8, 8, 8, 8, 8, 8)
CHUNKS = len(SIZES)
DIRECT = 6
VMEM = pl.BlockSpec(memory_space=pltpu.VMEM)
SMEM = pl.BlockSpec(memory_space=pltpu.SMEM)
HBM = pl.BlockSpec(memory_space=pltpu.HBM)
ANY = pl.BlockSpec(memory_space=pl.ANY)
PACE = 16 * 10**8
FIRST = 10**10
MIB = 1024 * 1024


def width_of(k, dims):
    return SIZES[k] * dims // sum(SIZES)


def columns_of(k, dims):
    unit = dims // sum(SIZES)
    left, right = sum(SIZES[:k]) * unit, sum(SIZES[k + 1 :]) * unit
    start = jnp.where(lax.axis_index("groups") == 0, left, right)
    return pl.ds(pl.multiple_of(start, unit), width_of(k, dims))


def products(rows, block):
    return lax.dot_general(
        rows, block, (((1,), (1,)), ((), ())), preferred_element_type=jnp.float32
    )


def scale_of(factor, counts, half, side):
    layer = lax.axis_index("layer")
    start = (layer if side else 1 - layer) * half
    index = start + lax.broadcasted_iota(jnp.int32, (half, 1), 0)
    return factor * (index < counts[0]).astype(jnp.float32)


def chunk_kernel(ks, queries, *refs):
    outs, sem = refs[-len(ks) - 1 : -1], refs[-1]
    dims = queries.shape[1]
    copies = [
        pltpu.make_async_copy(queries.at[:, columns_of(k, dims)], outs[i], sem.at[i])
        for i, k in enumerate(ks)
    ]
    for copy in copies:
        copy.start()
    for copy in copies:
        copy.wait()


def step_kernel(k, queries, received, *refs):
    out, sem = refs[-2:]
    even = lax.axis_index("dp") % 2 == 0
    own_copy = pltpu.make_async_copy(queries.at[:, columns_of(k, queries.shape[1])], out, sem)
    received_copy = pltpu.make_async_copy(received, out, sem)

    @pl.when(even)
    def _():
        own_copy.start()
        own_copy.wait()

    @pl.when(jnp.logical_not(even))
    def _():
        received_copy.start()
        received_copy.wait()


def own_kernel(pieces, factor, counts, documents, queries, eigenvalues, *refs):
    theirs, mine, held, inverse, sem = refs
    layer = lax.axis_index("layer")
    half = documents.shape[0] // 2
    dims = documents.shape[1]
    width = dims // pieces
    copies = {}
    for i in range(pieces):
        columns = pl.ds(i * width, width)
        for side, row in enumerate((1 - layer, layer)):
            copies[i, side] = pltpu.make_async_copy(
                documents.at[pl.ds(pl.multiple_of(row * half, half), half), columns],
                held.at[pl.ds(side * half, half), columns],
                sem.at[i, side],
            )
            copies[i, side].start()
    for start in range(0, dims, L_DIM):
        block = eigenvalues[:, start : start + L_DIM]
        damping = 0.1 * jnp.mean(block, axis=1, keepdims=True)
        inverse[:, start : start + L_DIM] = 1.0 / (block + damping)
    for i in range(pieces):
        columns = slice(i * width, (i + 1) * width)
        scaled = (queries[:, columns].astype(jnp.float32) * inverse[:, columns]).astype(jnp.bfloat16)
        for side, out in enumerate((theirs, mine)):
            copies[i, side].wait()
            term = products(held[side * half : (side + 1) * half, columns], scaled)
            if i == 0:
                out[...] = term
            else:
                out[...] += term
    theirs[...] *= scale_of(factor, counts, half, 0)
    mine[...] *= scale_of(factor, counts, half, 1)


def pair_kernel(ks, side, factor, fresh, counts, held, inverse, *refs):
    count = len(ks)
    chunks, out, block_buf = refs[: 2 * count], refs[-2], refs[-1]
    dims = inverse.shape[1]
    size = out.shape[0]
    first = 0 if side is None else side * size
    rows = chunks[0].shape[0]
    for i, k in enumerate(ks):
        columns = columns_of(k, dims)
        width = width_of(k, dims)
        for b in range(2):
            scaled = chunks[2 * i + b][...].astype(jnp.float32) * inverse[:, columns]
            block_buf[pl.ds(b * rows, rows), :width] = scaled.astype(jnp.bfloat16)
        term = products(held[first : first + size, columns], block_buf[:, :width])
        if i > 0:
            out[...] += term
        elif fresh:
            out[...] = term
        else:
            out[...] = refs[2 * count][first : first + size] + term
    if side is not None:
        out[...] *= scale_of(factor, counts, size, side)


def final_kernel(mine0, got0, mine, got, out):
    rows = mine0.shape[1]
    out[:, :rows] = mine0[...] + got0[...]
    out[:, rows:] = mine[...] + got[...]


def on_device(queries, documents, counts, eigenvalues):
    rows, dims = queries.shape
    doc_rows = documents.shape[0]
    half = doc_rows // 2
    owners = lax.axis_size("dp")
    factor = 1.0 / math.sqrt(dims * lax.axis_size("layer"))
    ahead = [(i, (i + 2) % owners) for i in range(owners)]
    pair = [(i, i ^ 1) for i in range(owners)]
    across = [(0, 1), (1, 0)]

    def chunk(k):
        return jax.ShapeDtypeStruct((rows, width_of(k, dims)), queries.dtype)

    def floats(*shape):
        return jax.ShapeDtypeStruct(shape, jnp.float32)

    def call(kernel, out_shape, in_specs, out_specs, scratch, vmem_mib=16, flops=PACE):
        return pl.pallas_call(
            kernel,
            out_shape=out_shape,
            in_specs=in_specs,
            out_specs=out_specs,
            scratch_shapes=scratch,
            compiler_params=pltpu.CompilerParams(vmem_limit_bytes=vmem_mib * MIB),
            cost_estimate=pl.CostEstimate(flops=flops, bytes_accessed=0, transcendentals=0),
        )

    def own_chunks(*ks, until=(), space=ANY, **options):
        return call(
            functools.partial(chunk_kernel, ks),
            [chunk(k) for k in ks],
            [ANY] * (1 + len(until)),
            [space] * len(ks),
            [pltpu.SemaphoreType.DMA((len(ks),))],
            **options,
        )(queries, *until)

    def step(k, *until):
        out = call(
            functools.partial(step_kernel, k),
            chunk(k),
            [ANY] * (2 + len(until)),
            ANY,
            [pltpu.SemaphoreType.DMA],
        )(queries, far[k], *until)
        near[k] = lax.ppermute(out, "dp", pair)
        return out

    def send_ahead(k, *until):
        (sent,) = own_chunks(k, until=until)
        far[k] = lax.ppermute(sent, "dp", ahead)
        return sent

    def pair_scores(*ks, sums=None, side=None, until=()):
        operands = [held, inverse] + [block[k] for k in ks for block in (near, far)]
        if sums is not None:
            operands.append(sums)
        return call(
            functools.partial(pair_kernel, ks, side, factor, sums is None),
            floats(doc_rows if side is None else half, 2 * rows),
            [SMEM] + [VMEM] * len(operands) + [ANY] * len(until),
            VMEM,
            [pltpu.VMEM((2 * rows, max(width_of(k, dims) for k in ks)), queries.dtype)],
        )(counts, *operands, *until)

    def send_across(block, k, *until):
        sent = lax.optimization_barrier((block[k], *until))[0]
        block[CHUNKS - 1 - k] = lax.ppermute(sent, "groups", across)

    far = [None] * CHUNKS
    near = [None] * CHUNKS

    sent = own_chunks(0, 1, space=VMEM, vmem_mib=53, flops=FIRST)
    for k in range(2):
        far[k] = lax.ppermute(sent[k], "dp", ahead)

    kept = lax.optimization_barrier((eigenvalues, sent[1]))[0].reshape(1, dims)
    pieces = 8
    theirs0, mine0, held, inverse = call(
        functools.partial(own_kernel, pieces, factor),
        [
            floats(half, rows),
            floats(half, rows),
            jax.ShapeDtypeStruct(documents.shape, documents.dtype),
            floats(1, dims),
        ],
        [SMEM, HBM, VMEM, VMEM],
        [VMEM] * 4,
        [pltpu.SemaphoreType.DMA((pieces, 2))],
        vmem_mib=40,
    )(counts, documents, queries, kept)

    out = step(0, inverse)
    out = send_ahead(2, out)
    send_across(far, 0, out)

    out = step(1, out)
    out = send_ahead(3, out)
    send_across(far, 1, out)
    sums = pair_scores(0, until=(out, far[7]))

    out = step(2, sums)
    out = send_ahead(4, out)
    send_across(near, 0, out)
    sums = pair_scores(1, sums=sums, until=(out, far[6]))

    out = step(3, sums)
    out = send_ahead(5, out)
    send_across(near, 1, out)
    sums = pair_scores(2, 7, sums=sums, until=(out,))

    out = step(4, sums)
    send_across(near, 2, out)
    got0 = lax.ppermute(lax.optimization_barrier((theirs0, out))[0], "layer", across)
    sums = pair_scores(3, 6, sums=sums, until=(out,))
    theirs = pair_scores(4, 5, sums=sums, side=0, until=(got0,))
    got = lax.ppermute(theirs, "layer", across)
    mine = pair_scores(4, 5, sums=sums, side=1, until=(theirs,))
    return call(final_kernel, floats(half, 3 * rows), [VMEM] * 4, VMEM, [])(mine0, got0, mine, got)


def solution(mesh):
    return jax.shard_map(
        on_device,
        mesh=mesh,
        in_specs=(P("dp", "layer"), P(("groups", "dp"), "layer"), P(("groups", "dp")), P("layer")),
        out_specs=P(("groups", "dp", "layer"), None),
        check_vma=False,
    )
```

```python
import functools
import math

import jax
import jax.numpy as jnp
from jax import lax
from jax.experimental import pallas as pl
from jax.experimental.pallas import tpu as pltpu
from jax.sharding import PartitionSpec as P

L_DIM = 8192
SIZES = (12, 12, 8, 8, 12, 12)
CHUNKS = len(SIZES)
DIRECT = 5
OWN_MIB = (44, 40)
VMEM = pl.BlockSpec(memory_space=pltpu.VMEM)
SMEM = pl.BlockSpec(memory_space=pltpu.SMEM)
HBM = pl.BlockSpec(memory_space=pltpu.HBM)
ANY = pl.BlockSpec(memory_space=pl.ANY)
PACE = 16 * 10**8
FIRST = 1024
MIB = 1024 * 1024


def width_of(k, dims):
    return SIZES[k] * dims // sum(SIZES)


def columns_of(k, dims, within=None):
    unit = dims // sum(SIZES)
    left, right = sum(SIZES[:k]), sum(SIZES[k + 1 :])
    if within:
        left, right = left % (sum(SIZES) // 2), right % (sum(SIZES) // 2)
    start = jnp.where(lax.axis_index("groups") == 0, left * unit, right * unit)
    return pl.ds(pl.multiple_of(start, unit), width_of(k, dims))


def half_columns(part, dims):
    group = lax.axis_index("groups")
    side = group if part == 0 else 1 - group
    return pl.ds(pl.multiple_of(side * (dims // 2), dims // 2), dims // 2)


def products(rows, block):
    return lax.dot_general(
        rows, block, (((1,), (1,)), ((), ())), preferred_element_type=jnp.float32
    )


def scale_of(factor, counts, half, side):
    layer = lax.axis_index("layer")
    start = (layer if side else 1 - layer) * half
    index = start + lax.broadcasted_iota(jnp.int32, (half, 1), 0)
    return factor * (index < counts[0]).astype(jnp.float32)


def chunk_kernel(ks, queries, *refs):
    outs, sem = refs[-len(ks) - 1 : -1], refs[-1]
    dims = queries.shape[1]
    copies = [
        pltpu.make_async_copy(queries.at[:, columns_of(k, dims)], outs[i], sem.at[i])
        for i, k in enumerate(ks)
    ]
    for copy in copies:
        copy.start()
    for copy in copies:
        copy.wait()


def step_kernel(k, queries, received, *refs):
    out, sem = refs[-2:]
    even = lax.axis_index("dp") % 2 == 0
    own_copy = pltpu.make_async_copy(queries.at[:, columns_of(k, queries.shape[1])], out, sem)
    received_copy = pltpu.make_async_copy(received, out, sem)

    @pl.when(even)
    def _():
        own_copy.start()
        own_copy.wait()

    @pl.when(jnp.logical_not(even))
    def _():
        received_copy.start()
        received_copy.wait()


def own_kernel(part, pieces, factor, counts, documents, queries, *refs):
    if part == 0:
        eigenvalues, theirs, mine, held, inverse, sem = refs[0], *refs[-5:]
        before = None
    else:
        inverse, before, theirs, mine, held, sem = refs[0], refs[1:3], *refs[-4:]
    layer = lax.axis_index("layer")
    half = documents.shape[0] // 2
    dims = documents.shape[1]
    width = dims // 2 // pieces
    first = half_columns(part, dims).start
    copies = []
    for i in range(pieces):
        start = pl.multiple_of(first + i * width, width)
        for at, row in enumerate((1 - layer, layer)):
            copies.append(
                pltpu.make_async_copy(
                    documents.at[pl.ds(pl.multiple_of(row * half, half), half), pl.ds(start, width)],
                    held.at[pl.ds(at * half, half), pl.ds(i * width, width)],
                    sem.at[i, at],
                )
            )
    for copy in copies:
        copy.start()
    if part == 0:
        for start in range(0, dims, L_DIM):
            block = eigenvalues[:, start : start + L_DIM]
            damping = 0.1 * jnp.mean(block, axis=1, keepdims=True)
            inverse[:, start : start + L_DIM] = 1.0 / (block + damping)
    for i in range(pieces):
        columns = pl.ds(pl.multiple_of(first + i * width, width), width)
        scaled = (queries[:, columns].astype(jnp.float32) * inverse[:, columns]).astype(jnp.bfloat16)
        copies[2 * i].wait()
        copies[2 * i + 1].wait()
        for side, out in enumerate((theirs, mine)):
            term = products(
                held[side * half : (side + 1) * half, i * width : (i + 1) * width], scaled
            )
            if i > 0:
                out[...] += term
            elif part == 0:
                out[...] = term
            else:
                out[...] = before[side][...] + term
    if part == 1:
        theirs[...] *= scale_of(factor, counts, half, 0)
        mine[...] *= scale_of(factor, counts, half, 1)


def held_of(k, held):
    return held[0] if k < CHUNKS // 2 else held[1]


def pair_kernel(ks, side, factor, fresh, counts, held0, held1, inverse, *refs):
    count = len(ks)
    chunks, out, block_buf = refs[: 2 * count], refs[-2], refs[-1]
    dims = inverse.shape[1]
    size = out.shape[0]
    first = 0 if side is None else side * size
    rows = chunks[0].shape[0]
    for i, k in enumerate(ks):
        width = width_of(k, dims)
        for b in range(2):
            scaled = chunks[2 * i + b][...].astype(jnp.float32) * inverse[:, columns_of(k, dims)]
            block_buf[pl.ds(b * rows, rows), :width] = scaled.astype(jnp.bfloat16)
        held = held_of(k, (held0, held1))
        term = products(held[first : first + size, columns_of(k, dims, True)], block_buf[:, :width])
        if i > 0:
            out[...] += term
        elif fresh:
            out[...] = term
        else:
            out[...] = refs[2 * count][first : first + size] + term
    if side is not None:
        out[...] *= scale_of(factor, counts, size, side)


def final_kernel(mine0, got0, mine, got, out):
    rows = mine0.shape[1]
    out[:, :rows] = mine0[...] + got0[...]
    out[:, rows:] = mine[...] + got[...]


def on_device(queries, documents, counts, eigenvalues):
    rows, dims = queries.shape
    doc_rows = documents.shape[0]
    half = doc_rows // 2
    owners = lax.axis_size("dp")
    factor = 1.0 / math.sqrt(dims * lax.axis_size("layer"))
    ahead = [(i, (i + 2) % owners) for i in range(owners)]
    pair = [(i, i ^ 1) for i in range(owners)]
    across = [(0, 1), (1, 0)]

    def chunk(k):
        return jax.ShapeDtypeStruct((rows, width_of(k, dims)), queries.dtype)

    def floats(*shape):
        return jax.ShapeDtypeStruct(shape, jnp.float32)

    def call(kernel, out_shape, in_specs, out_specs, scratch, vmem_mib=16, flops=PACE):
        return pl.pallas_call(
            kernel,
            out_shape=out_shape,
            in_specs=in_specs,
            out_specs=out_specs,
            scratch_shapes=scratch,
            compiler_params=pltpu.CompilerParams(vmem_limit_bytes=vmem_mib * MIB),
            cost_estimate=pl.CostEstimate(flops=flops, bytes_accessed=0, transcendentals=0),
        )

    def own_chunks(*ks, until=(), space=ANY, **options):
        return call(
            functools.partial(chunk_kernel, ks),
            [chunk(k) for k in ks],
            [ANY] * (1 + len(until)),
            [space] * len(ks),
            [pltpu.SemaphoreType.DMA((len(ks),))],
            **options,
        )(queries, *until)

    def step(k, *until):
        out = call(
            functools.partial(step_kernel, k),
            chunk(k),
            [ANY] * (2 + len(until)),
            ANY,
            [pltpu.SemaphoreType.DMA],
        )(queries, far[k], *until)
        near[k] = lax.ppermute(out, "dp", pair)
        return out

    def send_ahead(k, *until):
        (sent,) = own_chunks(k, until=until)
        far[k] = lax.ppermute(sent, "dp", ahead)
        return sent

    def pair_scores(*ks, sums=None, side=None, until=()):
        operands = [*held, inverse] + [block[k] for k in ks for block in (near, far)]
        if sums is not None:
            operands.append(sums)
        return call(
            functools.partial(pair_kernel, ks, side, factor, sums is None),
            floats(doc_rows if side is None else half, 2 * rows),
            [SMEM] + [VMEM] * len(operands) + [ANY] * len(until),
            VMEM,
            [pltpu.VMEM((2 * rows, max(width_of(k, dims) for k in ks)), queries.dtype)],
        )(counts, *operands, *until)

    def send_across(block, k, *until):
        sent = lax.optimization_barrier((block[k], *until))[0]
        block[CHUNKS - 1 - k] = lax.ppermute(sent, "groups", across)

    far = [None] * CHUNKS
    near = [None] * CHUNKS

    sent = own_chunks(0, 1, space=VMEM, vmem_mib=53, flops=FIRST)
    for k in range(2):
        far[k] = lax.ppermute(sent[k], "dp", ahead)

    def own_scores(part, *operands, until=()):
        pieces = 4
        outs = [
            floats(half, rows),
            floats(half, rows),
            jax.ShapeDtypeStruct((doc_rows, dims // 2), documents.dtype),
            floats(1, dims),
        ][: 4 - part]
        return call(
            functools.partial(own_kernel, part, pieces, factor),
            outs,
            [SMEM, HBM] + [VMEM] * (1 + len(operands)) + [ANY] * len(until),
            [VMEM] * len(outs),
            [pltpu.SemaphoreType.DMA((pieces, 2))],
            vmem_mib=OWN_MIB[part],
        )(counts, documents, queries, *operands, *until)

    kept = lax.optimization_barrier((eigenvalues, sent[1]))[0].reshape(1, dims)
    theirs0, mine0, held0, inverse = own_scores(0, kept)

    out = step(0, inverse)
    out = send_ahead(2, out)
    send_across(far, 0, out)
    theirs0, mine0, held1 = own_scores(1, inverse, theirs0, mine0, until=(out,))
    held = held0, held1

    out = step(1, theirs0)
    out = send_ahead(3, out)
    send_across(near, 0, out)
    sums = pair_scores(0, until=(out, far[5]))

    out = step(2, sums)
    out = send_ahead(4, out)
    send_across(near, 1, out)
    sums = pair_scores(1, sums=sums, until=(out,))

    out = step(3, sums)
    got0 = lax.ppermute(lax.optimization_barrier((theirs0, out))[0], "layer", across)
    sums = pair_scores(2, 5, sums=sums, until=(out,))
    theirs = pair_scores(3, 4, sums=sums, side=0, until=(got0,))
    got = lax.ppermute(theirs, "layer", across)
    mine = pair_scores(3, 4, sums=sums, side=1, until=(theirs,))
    return call(final_kernel, floats(half, 3 * rows), [VMEM] * 4, VMEM, [])(mine0, got0, mine, got)


def solution(mesh):
    return jax.shard_map(
        on_device,
        mesh=mesh,
        in_specs=(P("dp", "layer"), P(("groups", "dp"), "layer"), P(("groups", "dp")), P("layer")),
        out_specs=P(("groups", "dp", "layer"), None),
        check_vma=False,
    )
```

```python
import functools
import math

import jax
import jax.numpy as jnp
from jax import lax
from jax.experimental import pallas as pl
from jax.experimental.pallas import tpu as pltpu
from jax.sharding import PartitionSpec as P

L_DIM = 8192
SIZES = (12, 12, 8, 8, 12, 12)
CHUNKS = len(SIZES)
DIRECT = 5
OWN_MIB = (44, 40)
VMEM = pl.BlockSpec(memory_space=pltpu.VMEM)
SMEM = pl.BlockSpec(memory_space=pltpu.SMEM)
HBM = pl.BlockSpec(memory_space=pltpu.HBM)
ANY = pl.BlockSpec(memory_space=pl.ANY)
PACE = 16 * 10**8
FIRST = 1024
MIB = 1024 * 1024


def width_of(k, dims):
    return SIZES[k] * dims // sum(SIZES)


def columns_of(k, dims, within=None):
    unit = dims // sum(SIZES)
    left, right = sum(SIZES[:k]), sum(SIZES[k + 1 :])
    if within:
        left, right = left % (sum(SIZES) // 2), right % (sum(SIZES) // 2)
    start = jnp.where(lax.axis_index("groups") == 0, left * unit, right * unit)
    return pl.ds(pl.multiple_of(start, unit), width_of(k, dims))


def half_columns(part, dims):
    group = lax.axis_index("groups")
    side = group if part == 0 else 1 - group
    return pl.ds(pl.multiple_of(side * (dims // 2), dims // 2), dims // 2)


def products(rows, block):
    return lax.dot_general(
        rows, block, (((1,), (1,)), ((), ())), preferred_element_type=jnp.float32
    )


def scale_of(factor, counts, half, side):
    layer = lax.axis_index("layer")
    start = (layer if side else 1 - layer) * half
    index = start + lax.broadcasted_iota(jnp.int32, (half, 1), 0)
    return factor * (index < counts[0]).astype(jnp.float32)


def chunk_kernel(ks, queries, *refs):
    outs, sem = refs[-len(ks) - 1 : -1], refs[-1]
    dims = queries.shape[1]
    copies = [
        pltpu.make_async_copy(queries.at[:, columns_of(k, dims)], outs[i], sem.at[i])
        for i, k in enumerate(ks)
    ]
    for copy in copies:
        copy.start()
    for copy in copies:
        copy.wait()


def step_kernel(k, queries, received, *refs):
    out, sem = refs[-2:]
    even = lax.axis_index("dp") % 2 == 0
    own_copy = pltpu.make_async_copy(queries.at[:, columns_of(k, queries.shape[1])], out, sem)
    received_copy = pltpu.make_async_copy(received, out, sem)

    @pl.when(even)
    def _():
        own_copy.start()
        own_copy.wait()

    @pl.when(jnp.logical_not(even))
    def _():
        received_copy.start()
        received_copy.wait()


def own_kernel(part, pieces, factor, counts, documents, queries, *refs):
    if part == 0:
        eigenvalues, theirs, mine, held, inverse, sem = refs[0], *refs[-5:]
        before = None
    else:
        inverse, before, theirs, mine, held, sem = refs[0], refs[1:3], *refs[-4:]
    layer = lax.axis_index("layer")
    half = documents.shape[0] // 2
    dims = documents.shape[1]
    width = dims // 2 // pieces
    first = half_columns(part, dims).start
    copies = []
    for i in range(pieces):
        start = pl.multiple_of(first + i * width, width)
        for at, row in enumerate((1 - layer, layer)):
            copies.append(
                pltpu.make_async_copy(
                    documents.at[pl.ds(pl.multiple_of(row * half, half), half), pl.ds(start, width)],
                    held.at[pl.ds(at * half, half), pl.ds(i * width, width)],
                    sem.at[i, at],
                )
            )
    for copy in copies:
        copy.start()
    if part == 0:
        for start in range(0, dims, L_DIM):
            block = eigenvalues[:, start : start + L_DIM]
            damping = 0.1 * jnp.mean(block, axis=1, keepdims=True)
            inverse[:, start : start + L_DIM] = 1.0 / (block + damping)
    for i in range(pieces):
        columns = pl.ds(pl.multiple_of(first + i * width, width), width)
        scaled = (queries[:, columns].astype(jnp.float32) * inverse[:, columns]).astype(jnp.bfloat16)
        copies[2 * i].wait()
        copies[2 * i + 1].wait()
        for side, out in enumerate((theirs, mine)):
            term = products(
                held[side * half : (side + 1) * half, i * width : (i + 1) * width], scaled
            )
            if i > 0:
                out[...] += term
            elif part == 0:
                out[...] = term
            else:
                out[...] = before[side][...] + term
    if part == 1:
        theirs[...] *= scale_of(factor, counts, half, 0)
        mine[...] *= scale_of(factor, counts, half, 1)


def held_of(k, held):
    return held[0] if k < CHUNKS // 2 else held[1]


def one_product(k, rows, held, inverse, chunk):
    dims = inverse.shape[1]
    scaled = chunk[...].astype(jnp.float32) * inverse[:, columns_of(k, dims)]
    return products(held_of(k, held)[rows, columns_of(k, dims, True)], scaled.astype(jnp.bfloat16))


def pair_kernel(ks, alone, fresh, held0, held1, inverse, *refs):
    count = len(ks)
    chunks, out, block_buf = refs[: 2 * count], refs[-2], refs[-1]
    dims = inverse.shape[1]
    rows = chunks[0].shape[0]
    for i, k in enumerate(ks):
        width = width_of(k, dims)
        for b in range(2):
            scaled = chunks[2 * i + b][...].astype(jnp.float32) * inverse[:, columns_of(k, dims)]
            block_buf[pl.ds(b * rows, rows), :width] = scaled.astype(jnp.bfloat16)
        held = held_of(k, (held0, held1))
        term = products(held[:, columns_of(k, dims, True)], block_buf[:, :width])
        if i > 0:
            out[...] += term
        elif fresh:
            out[...] = term
        else:
            out[...] = refs[2 * count][...] + term
    if alone is not None:
        out[:, rows:] += one_product(
            alone, slice(None), (held0, held1), inverse, refs[2 * count + 1 - fresh]
        )


def far_kernel(k, factor, counts, held0, held1, inverse, near, far, sums, *outs):
    near_out, theirs, mine, block = outs
    dims = inverse.shape[1]
    rows = near.shape[0]
    half = mine.shape[0]
    held = held_of(k, (held0, held1))
    for b, chunk in enumerate((near, far)):
        scaled = chunk[...].astype(jnp.float32) * inverse[:, columns_of(k, dims)]
        block[b * rows : (b + 1) * rows, :] = scaled.astype(jnp.bfloat16)
    for side, out in enumerate((theirs, mine)):
        part = slice(side * half, (side + 1) * half)
        total = sums[part] + products(held[part, columns_of(k, dims, True)], block[...])
        near_out[part] = total[:, :rows]
        out[...] = total[:, rows:] * scale_of(factor, counts, half, side)


def near_kernel(k, side, factor, counts, held0, held1, inverse, last, near, *refs):
    out = refs[-1]
    half = out.shape[0]
    part = slice(side * half, (side + 1) * half)
    total = near[part] + one_product(k, part, (held0, held1), inverse, last)
    out[...] = total * scale_of(factor, counts, half, side)


def final_kernel(*refs):
    terms, out = refs[:-1], refs[-1]
    rows = terms[0].shape[1]
    for i in range(3):
        out[:, i * rows : (i + 1) * rows] = terms[2 * i][...] + terms[2 * i + 1][...]


def on_device(queries, documents, counts, eigenvalues):
    rows, dims = queries.shape
    doc_rows = documents.shape[0]
    half = doc_rows // 2
    owners = lax.axis_size("dp")
    factor = 1.0 / math.sqrt(dims * lax.axis_size("layer"))
    ahead = [(i, (i + 2) % owners) for i in range(owners)]
    pair = [(i, i ^ 1) for i in range(owners)]
    across = [(0, 1), (1, 0)]

    def chunk(k):
        return jax.ShapeDtypeStruct((rows, width_of(k, dims)), queries.dtype)

    def floats(*shape):
        return jax.ShapeDtypeStruct(shape, jnp.float32)

    def call(kernel, out_shape, in_specs, out_specs, scratch, vmem_mib=16, flops=PACE):
        return pl.pallas_call(
            kernel,
            out_shape=out_shape,
            in_specs=in_specs,
            out_specs=out_specs,
            scratch_shapes=scratch,
            compiler_params=pltpu.CompilerParams(vmem_limit_bytes=vmem_mib * MIB),
            cost_estimate=pl.CostEstimate(flops=flops, bytes_accessed=0, transcendentals=0),
        )

    def own_chunks(*ks, until=(), space=ANY, **options):
        return call(
            functools.partial(chunk_kernel, ks),
            [chunk(k) for k in ks],
            [ANY] * (1 + len(until)),
            [space] * len(ks),
            [pltpu.SemaphoreType.DMA((len(ks),))],
            **options,
        )(queries, *until)

    def step(k, *until):
        out = call(
            functools.partial(step_kernel, k),
            chunk(k),
            [ANY] * (2 + len(until)),
            ANY,
            [pltpu.SemaphoreType.DMA],
        )(queries, far[k], *until)
        near[k] = lax.ppermute(out, "dp", pair)
        return out

    def send_ahead(k, *until):
        (sent,) = own_chunks(k, until=until)
        far[k] = lax.ppermute(sent, "dp", ahead)
        return sent

    def pair_scores(*ks, sums=None, alone=None, until=()):
        operands = [*held, inverse] + [block[k] for k in ks for block in (near, far)]
        if sums is not None:
            operands.append(sums)
        if alone is not None:
            operands.append(far[alone])
        return call(
            functools.partial(pair_kernel, ks, alone, sums is None),
            floats(doc_rows, 2 * rows),
            [VMEM] * len(operands) + [ANY] * len(until),
            VMEM,
            [pltpu.VMEM((2 * rows, max(width_of(k, dims) for k in ks)), queries.dtype)],
        )(*operands, *until)

    def send_across(block, k, *until):
        sent = lax.optimization_barrier((block[k], *until))[0]
        block[CHUNKS - 1 - k] = lax.ppermute(sent, "groups", across)

    far = [None] * CHUNKS
    near = [None] * CHUNKS

    sent = own_chunks(0, 1, space=VMEM, vmem_mib=53, flops=FIRST)
    for k in range(2):
        far[k] = lax.ppermute(sent[k], "dp", ahead)

    def own_scores(part, *operands, until=()):
        pieces = 4
        outs = [
            floats(half, rows),
            floats(half, rows),
            jax.ShapeDtypeStruct((doc_rows, dims // 2), documents.dtype),
            floats(1, dims),
        ][: 4 - part]
        return call(
            functools.partial(own_kernel, part, pieces, factor),
            outs,
            [SMEM, HBM] + [VMEM] * (1 + len(operands)) + [ANY] * len(until),
            [VMEM] * len(outs),
            [pltpu.SemaphoreType.DMA((pieces, 2))],
            vmem_mib=OWN_MIB[part],
        )(counts, documents, queries, *operands, *until)

    kept = lax.optimization_barrier((eigenvalues, sent[1]))[0].reshape(1, dims)
    theirs0, mine0, held0, inverse = own_scores(0, kept)

    out = step(0, inverse)
    out = send_ahead(2, out)
    send_across(far, 0, out)
    theirs0, mine0, held1 = own_scores(1, inverse, theirs0, mine0, until=(out,))
    held = held0, held1

    out = step(1, theirs0)
    out = send_ahead(3, out)
    send_across(near, 0, out)
    sums = pair_scores(0, until=(out, far[5]))

    out = step(2, sums)
    out = send_ahead(4, out)
    send_across(near, 1, out)
    sums = pair_scores(1, sums=sums, until=(out,))

    out = step(3, sums)
    got0 = lax.ppermute(lax.optimization_barrier((theirs0, out))[0], "layer", across)
    sums = pair_scores(2, 5, sums=sums, alone=3, until=(out,))
    near_sums, theirs_far, mine_far = call(
        functools.partial(far_kernel, 4, factor),
        [floats(doc_rows, rows), floats(half, rows), floats(half, rows)],
        [SMEM] + [VMEM] * 6,
        [VMEM] * 3,
        [pltpu.VMEM((2 * rows, width_of(4, dims)), queries.dtype)],
    )(counts, *held, inverse, near[4], far[4], sums)
    got_far = lax.ppermute(theirs_far, "layer", across)

    def near_scores(side, *until):
        return call(
            functools.partial(near_kernel, 3, side, factor),
            floats(half, rows),
            [SMEM] + [VMEM] * 5 + [ANY] * len(until),
            VMEM,
            [],
        )(counts, *held, inverse, near[3], near_sums, *until)

    theirs_near = near_scores(0, got0, got_far)
    got_near = lax.ppermute(theirs_near, "layer", across)
    mine_near = near_scores(1, theirs_near)
    return call(final_kernel, floats(half, 3 * rows), [VMEM] * 6, VMEM, [])(
        mine0, got0, mine_near, got_near, mine_far, got_far
    )


def solution(mesh):
    return jax.shard_map(
        on_device,
        mesh=mesh,
        in_specs=(P("dp", "layer"), P(("groups", "dp"), "layer"), P(("groups", "dp")), P("layer")),
        out_specs=P(("groups", "dp", "layer"), None),
        check_vma=False,
    )
```

```python
import functools
import math

import jax
import jax.numpy as jnp
from jax import lax
from jax.experimental import pallas as pl
from jax.experimental.pallas import tpu as pltpu
from jax.sharding import PartitionSpec as P

L_DIM = 8192
SIZES = (12, 12, 8, 8, 12, 12)
CHUNKS = len(SIZES)
DIRECT = 5
OWN_MIB = (44, 40)
VMEM = pl.BlockSpec(memory_space=pltpu.VMEM)
SMEM = pl.BlockSpec(memory_space=pltpu.SMEM)
HBM = pl.BlockSpec(memory_space=pltpu.HBM)
ANY = pl.BlockSpec(memory_space=pl.ANY)
PACE = 16 * 10**8
FIRST = 1024
MIB = 1024 * 1024


def width_of(k, dims):
    return SIZES[k] * dims // sum(SIZES)


def columns_of(k, dims, within=None):
    unit = dims // sum(SIZES)
    left, right = sum(SIZES[:k]), sum(SIZES[k + 1 :])
    if within:
        left, right = left % (sum(SIZES) // 2), right % (sum(SIZES) // 2)
    start = jnp.where(lax.axis_index("groups") == 0, left * unit, right * unit)
    return pl.ds(pl.multiple_of(start, unit), width_of(k, dims))


def half_columns(part, dims):
    group = lax.axis_index("groups")
    side = group if part == 0 else 1 - group
    return pl.ds(pl.multiple_of(side * (dims // 2), dims // 2), dims // 2)


def products(rows, block):
    return lax.dot_general(
        rows, block, (((1,), (1,)), ((), ())), preferred_element_type=jnp.float32
    )


def scale_of(factor, counts, half, side):
    layer = lax.axis_index("layer")
    start = (layer if side else 1 - layer) * half
    index = start + lax.broadcasted_iota(jnp.int32, (half, 1), 0)
    return factor * (index < counts[0]).astype(jnp.float32)


def chunk_kernel(ks, queries, *refs):
    outs, sem = refs[-len(ks) - 1 : -1], refs[-1]
    dims = queries.shape[1]
    copies = [
        pltpu.make_async_copy(queries.at[:, columns_of(k, dims)], outs[i], sem.at[i])
        for i, k in enumerate(ks)
    ]
    for copy in copies:
        copy.start()
    for copy in copies:
        copy.wait()


def step_kernel(k, queries, received, *refs):
    out, sem = refs[-2:]
    even = lax.axis_index("dp") % 2 == 0
    own_copy = pltpu.make_async_copy(queries.at[:, columns_of(k, queries.shape[1])], out, sem)
    received_copy = pltpu.make_async_copy(received, out, sem)

    @pl.when(even)
    def _():
        own_copy.start()
        own_copy.wait()

    @pl.when(jnp.logical_not(even))
    def _():
        received_copy.start()
        received_copy.wait()


def own_kernel(part, pieces, factor, counts, documents, queries, *refs):
    if part == 0:
        eigenvalues, theirs, mine, held, inverse, sem = refs[0], *refs[-5:]
        before = None
    else:
        inverse, before, theirs, mine, held, sem = refs[0], refs[1:3], *refs[-4:]
    layer = lax.axis_index("layer")
    half = documents.shape[0] // 2
    dims = documents.shape[1]
    width = dims // 2 // pieces
    first = half_columns(part, dims).start
    copies = []
    for i in range(pieces):
        start = pl.multiple_of(first + i * width, width)
        for at, row in enumerate((1 - layer, layer)):
            copies.append(
                pltpu.make_async_copy(
                    documents.at[pl.ds(pl.multiple_of(row * half, half), half), pl.ds(start, width)],
                    held.at[pl.ds(at * half, half), pl.ds(i * width, width)],
                    sem.at[i, at],
                )
            )
    for copy in copies:
        copy.start()
    if part == 0:
        for start in range(0, dims, L_DIM):
            block = eigenvalues[:, start : start + L_DIM]
            damping = 0.1 * jnp.mean(block, axis=1, keepdims=True)
            inverse[:, start : start + L_DIM] = 1.0 / (block + damping)
    for i in range(pieces):
        columns = pl.ds(pl.multiple_of(first + i * width, width), width)
        scaled = (queries[:, columns].astype(jnp.float32) * inverse[:, columns]).astype(jnp.bfloat16)
        copies[2 * i].wait()
        copies[2 * i + 1].wait()
        for side, out in enumerate((theirs, mine)):
            term = products(
                held[side * half : (side + 1) * half, i * width : (i + 1) * width], scaled
            )
            if i > 0:
                out[...] += term
            elif part == 0:
                out[...] = term
            else:
                out[...] = before[side][...] + term
    if part == 1:
        theirs[...] *= scale_of(factor, counts, half, 0)
        mine[...] *= scale_of(factor, counts, half, 1)


def held_of(k, held):
    return held[0] if k < CHUNKS // 2 else held[1]


def one_product(k, rows, held, inverse, chunk):
    dims = inverse.shape[1]
    scaled = chunk[...].astype(jnp.float32) * inverse[:, columns_of(k, dims)]
    return products(held_of(k, held)[rows, columns_of(k, dims, True)], scaled.astype(jnp.bfloat16))


def pair_kernel(ks, alone, fresh, held0, held1, inverse, *refs):
    count = len(ks)
    chunks, out, block_buf = refs[: 2 * count], refs[-2], refs[-1]
    dims = inverse.shape[1]
    rows = chunks[0].shape[0]
    for i, k in enumerate(ks):
        width = width_of(k, dims)
        for b in range(2):
            scaled = chunks[2 * i + b][...].astype(jnp.float32) * inverse[:, columns_of(k, dims)]
            block_buf[pl.ds(b * rows, rows), :width] = scaled.astype(jnp.bfloat16)
        held = held_of(k, (held0, held1))
        term = products(held[:, columns_of(k, dims, True)], block_buf[:, :width])
        if i > 0:
            out[...] += term
        elif fresh:
            out[...] = term
        else:
            out[...] = refs[2 * count][...] + term
    if alone is not None:
        out[:, rows:] += one_product(
            alone, slice(None), (held0, held1), inverse, refs[2 * count + 1 - fresh]
        )


def far_kernel(k, factor, counts, held0, held1, inverse, near, far, sums, *outs):
    near_out, theirs, mine, block = outs
    dims = inverse.shape[1]
    rows = near.shape[0]
    half = mine.shape[0]
    held = held_of(k, (held0, held1))
    for b, chunk in enumerate((near, far)):
        scaled = chunk[...].astype(jnp.float32) * inverse[:, columns_of(k, dims)]
        block[b * rows : (b + 1) * rows, :] = scaled.astype(jnp.bfloat16)
    for side, out in enumerate((theirs, mine)):
        part = slice(side * half, (side + 1) * half)
        total = sums[part] + products(held[part, columns_of(k, dims, True)], block[...])
        near_out[part] = total[:, :rows]
        out[...] = total[:, rows:] * scale_of(factor, counts, half, side)


def near_kernel(k, side, factor, counts, held0, held1, inverse, last, near, *refs):
    out = refs[-1]
    half = out.shape[0]
    part = slice(side * half, (side + 1) * half)
    total = near[part] + one_product(k, part, (held0, held1), inverse, last)
    out[...] = total * scale_of(factor, counts, half, side)


def final_kernel(*refs):
    terms, out = refs[:-1], refs[-1]
    rows = terms[0].shape[1]
    for i in range(3):
        out[:, i * rows : (i + 1) * rows] = terms[2 * i][...] + terms[2 * i + 1][...]


def on_device(queries, documents, counts, eigenvalues):
    rows, dims = queries.shape
    doc_rows = documents.shape[0]
    half = doc_rows // 2
    owners = lax.axis_size("dp")
    factor = 1.0 / math.sqrt(dims * lax.axis_size("layer"))
    ahead = [(i, (i + 2) % owners) for i in range(owners)]
    pair = [(i, i ^ 1) for i in range(owners)]
    across = [(0, 1), (1, 0)]

    def chunk(k):
        return jax.ShapeDtypeStruct((rows, width_of(k, dims)), queries.dtype)

    def floats(*shape):
        return jax.ShapeDtypeStruct(shape, jnp.float32)

    def call(kernel, out_shape, in_specs, out_specs, scratch, vmem_mib=16, flops=PACE):
        return pl.pallas_call(
            kernel,
            out_shape=out_shape,
            in_specs=in_specs,
            out_specs=out_specs,
            scratch_shapes=scratch,
            compiler_params=pltpu.CompilerParams(vmem_limit_bytes=vmem_mib * MIB),
            cost_estimate=pl.CostEstimate(flops=flops, bytes_accessed=0, transcendentals=0),
        )

    def own_chunks(*ks, until=(), space=ANY, **options):
        return call(
            functools.partial(chunk_kernel, ks),
            [chunk(k) for k in ks],
            [ANY] * (1 + len(until)),
            [space] * len(ks),
            [pltpu.SemaphoreType.DMA((len(ks),))],
            **options,
        )(queries, *until)

    def step(k, *until):
        out = call(
            functools.partial(step_kernel, k),
            chunk(k),
            [ANY] * (2 + len(until)),
            ANY,
            [pltpu.SemaphoreType.DMA],
        )(queries, far[k], *until)
        near[k] = lax.ppermute(out, "dp", pair)
        return out

    def send_ahead(k, *until):
        (sent,) = own_chunks(k, until=until)
        far[k] = lax.ppermute(sent, "dp", ahead)
        return sent

    def pair_scores(*ks, sums=None, alone=None, until=()):
        operands = [*held, inverse] + [block[k] for k in ks for block in (near, far)]
        if sums is not None:
            operands.append(sums)
        if alone is not None:
            operands.append(far[alone])
        return call(
            functools.partial(pair_kernel, ks, alone, sums is None),
            floats(doc_rows, 2 * rows),
            [VMEM] * len(operands) + [ANY] * len(until),
            VMEM,
            [pltpu.VMEM((2 * rows, max(width_of(k, dims) for k in ks)), queries.dtype)],
        )(*operands, *until)

    def send_across(block, k, *until):
        sent = lax.optimization_barrier((block[k], *until))[0]
        block[CHUNKS - 1 - k] = lax.ppermute(sent, "groups", across)

    far = [None] * CHUNKS
    near = [None] * CHUNKS

    sent = own_chunks(0, 1, space=VMEM, vmem_mib=53, flops=FIRST)
    for k in range(2):
        far[k] = lax.ppermute(sent[k], "dp", ahead)

    def own_scores(part, *operands, until=()):
        pieces = 4
        outs = [
            floats(half, rows),
            floats(half, rows),
            jax.ShapeDtypeStruct((doc_rows, dims // 2), documents.dtype),
            floats(1, dims),
        ][: 4 - part]
        return call(
            functools.partial(own_kernel, part, pieces, factor),
            outs,
            [SMEM, HBM] + [VMEM] * (1 + len(operands)) + [ANY] * len(until),
            [VMEM] * len(outs),
            [pltpu.SemaphoreType.DMA((pieces, 2))],
            vmem_mib=OWN_MIB[part],
        )(counts, documents, queries, *operands, *until)

    kept = lax.optimization_barrier((eigenvalues, sent[1]))[0].reshape(1, dims)
    theirs0, mine0, held0, inverse = own_scores(0, kept)

    out = step(0, inverse)
    out = send_ahead(2, out)
    send_across(far, 0, out)
    theirs0, mine0, held1 = own_scores(1, inverse, theirs0, mine0, until=(out,))
    held = held0, held1

    out = step(1, theirs0)
    out = send_ahead(3, out)
    send_across(near, 0, out)
    sums = pair_scores(0, until=(out, far[5]))

    out = step(2, sums)
    out = send_ahead(4, out)
    send_across(near, 1, out)
    sums = pair_scores(1, sums=sums, until=(out,))

    out = step(3, sums)
    got0 = lax.ppermute(lax.optimization_barrier((theirs0, out))[0], "layer", across)
    sums = pair_scores(2, 5, sums=sums, alone=3, until=(out,))
    near_sums, theirs_far, mine_far = call(
        functools.partial(far_kernel, 4, factor),
        [floats(doc_rows, rows), floats(half, rows), floats(half, rows)],
        [SMEM] + [VMEM] * 6,
        [VMEM] * 3,
        [pltpu.VMEM((2 * rows, width_of(4, dims)), queries.dtype)],
    )(counts, *held, inverse, near[4], far[4], sums)
    got_far = lax.ppermute(theirs_far, "layer", across)

    def near_scores(side, *until):
        return call(
            functools.partial(near_kernel, 3, side, factor),
            floats(half, rows),
            [SMEM] + [VMEM] * 5 + [ANY] * len(until),
            VMEM,
            [],
        )(counts, *held, inverse, near[3], near_sums, *until)

    theirs_near = near_scores(0, got0)
    got_near = lax.ppermute(theirs_near, "layer", across)
    mine_near = near_scores(1, theirs_near, got_far)
    return call(final_kernel, floats(half, 3 * rows), [VMEM] * 6, VMEM, [])(
        mine0, got0, mine_near, got_near, mine_far, got_far
    )


def solution(mesh):
    return jax.shard_map(
        on_device,
        mesh=mesh,
        in_specs=(P("dp", "layer"), P(("groups", "dp"), "layer"), P(("groups", "dp")), P("layer")),
        out_specs=P(("groups", "dp", "layer"), None),
        check_vma=False,
    )
```

```python
import functools
import math

import jax
import jax.numpy as jnp
from jax import lax
from jax.experimental import pallas as pl
from jax.experimental.pallas import tpu as pltpu
from jax.sharding import PartitionSpec as P

L_DIM = 8192
SIZES = (12, 12, 8, 8, 12, 12)
CHUNKS = len(SIZES)
DIRECT = 5
OWN_MIB = (44, 40)
VMEM = pl.BlockSpec(memory_space=pltpu.VMEM)
SMEM = pl.BlockSpec(memory_space=pltpu.SMEM)
HBM = pl.BlockSpec(memory_space=pltpu.HBM)
ANY = pl.BlockSpec(memory_space=pl.ANY)
PACE = 16 * 10**8
FIRST = 1024
MIB = 1024 * 1024


def width_of(k, dims):
    return SIZES[k] * dims // sum(SIZES)


def columns_of(k, dims, within=None):
    unit = dims // sum(SIZES)
    left, right = sum(SIZES[:k]), sum(SIZES[k + 1 :])
    if within:
        left, right = left % (sum(SIZES) // 2), right % (sum(SIZES) // 2)
    start = jnp.where(lax.axis_index("groups") == 0, left * unit, right * unit)
    return pl.ds(pl.multiple_of(start, unit), width_of(k, dims))


def half_columns(part, dims):
    group = lax.axis_index("groups")
    side = group if part == 0 else 1 - group
    return pl.ds(pl.multiple_of(side * (dims // 2), dims // 2), dims // 2)


def products(rows, block):
    return lax.dot_general(
        rows, block, (((1,), (1,)), ((), ())), preferred_element_type=jnp.float32
    )


def scale_of(factor, counts, half, side):
    layer = lax.axis_index("layer")
    start = (layer if side else 1 - layer) * half
    index = start + lax.broadcasted_iota(jnp.int32, (half, 1), 0)
    return factor * (index < counts[0]).astype(jnp.float32)


def chunk_kernel(ks, queries, *refs):
    outs, sem = refs[-len(ks) - 1 : -1], refs[-1]
    dims = queries.shape[1]
    copies = [
        pltpu.make_async_copy(queries.at[:, columns_of(k, dims)], outs[i], sem.at[i])
        for i, k in enumerate(ks)
    ]
    for copy in copies:
        copy.start()
    for copy in copies:
        copy.wait()


def step_kernel(k, queries, received, *refs):
    out, sem = refs[-2:]
    even = lax.axis_index("dp") % 2 == 0
    own_copy = pltpu.make_async_copy(queries.at[:, columns_of(k, queries.shape[1])], out, sem)
    received_copy = pltpu.make_async_copy(received, out, sem)

    @pl.when(even)
    def _():
        own_copy.start()
        own_copy.wait()

    @pl.when(jnp.logical_not(even))
    def _():
        received_copy.start()
        received_copy.wait()


def own_kernel(part, pieces, factor, counts, documents, queries, *refs):
    if part == 0:
        eigenvalues, theirs, mine, held, inverse, sem = refs[0], *refs[-5:]
        before = None
    else:
        inverse, before, theirs, mine, held, sem = refs[0], refs[1:3], *refs[-4:]
    layer = lax.axis_index("layer")
    half = documents.shape[0] // 2
    dims = documents.shape[1]
    width = dims // 2 // pieces
    first = half_columns(part, dims).start
    copies = []
    for i in range(pieces):
        start = pl.multiple_of(first + i * width, width)
        for at, row in enumerate((1 - layer, layer)):
            copies.append(
                pltpu.make_async_copy(
                    documents.at[pl.ds(pl.multiple_of(row * half, half), half), pl.ds(start, width)],
                    held.at[pl.ds(at * half, half), pl.ds(i * width, width)],
                    sem.at[i, at],
                )
            )
    for copy in copies:
        copy.start()
    if part == 0:
        for start in range(0, dims, L_DIM):
            block = eigenvalues[:, start : start + L_DIM]
            damping = 0.1 * jnp.mean(block, axis=1, keepdims=True)
            inverse[:, start : start + L_DIM] = 1.0 / (block + damping)
    for i in range(pieces):
        columns = pl.ds(pl.multiple_of(first + i * width, width), width)
        scaled = (queries[:, columns].astype(jnp.float32) * inverse[:, columns]).astype(jnp.bfloat16)
        copies[2 * i].wait()
        copies[2 * i + 1].wait()
        for side, out in enumerate((theirs, mine)):
            term = products(
                held[side * half : (side + 1) * half, i * width : (i + 1) * width], scaled
            )
            if i > 0:
                out[...] += term
            elif part == 0:
                out[...] = term
            else:
                out[...] = before[side][...] + term
    if part == 1:
        theirs[...] *= scale_of(factor, counts, half, 0)
        mine[...] *= scale_of(factor, counts, half, 1)


def held_of(k, held):
    return held[0] if k < CHUNKS // 2 else held[1]


def one_product(k, rows, held, inverse, chunk):
    dims = inverse.shape[1]
    scaled = chunk[...].astype(jnp.float32) * inverse[:, columns_of(k, dims)]
    return products(held_of(k, held)[rows, columns_of(k, dims, True)], scaled.astype(jnp.bfloat16))


def pair_kernel(ks, alone, fresh, held0, held1, inverse, *refs):
    count = len(ks)
    chunks, out, block_buf = refs[: 2 * count], refs[-2], refs[-1]
    dims = inverse.shape[1]
    rows = chunks[0].shape[0]
    for i, k in enumerate(ks):
        width = width_of(k, dims)
        for b in range(2):
            scaled = chunks[2 * i + b][...].astype(jnp.float32) * inverse[:, columns_of(k, dims)]
            block_buf[pl.ds(b * rows, rows), :width] = scaled.astype(jnp.bfloat16)
        held = held_of(k, (held0, held1))
        term = products(held[:, columns_of(k, dims, True)], block_buf[:, :width])
        if i > 0:
            out[...] += term
        elif fresh:
            out[...] = term
        else:
            out[...] = refs[2 * count][...] + term
    if alone is not None:
        out[:, rows:] += one_product(
            alone, slice(None), (held0, held1), inverse, refs[2 * count + 1 - fresh]
        )


def far_kernel(k, factor, counts, held0, held1, inverse, near, far, sums, *outs):
    near_out, theirs, mine, block = outs
    dims = inverse.shape[1]
    rows = near.shape[0]
    half = mine.shape[0]
    held = held_of(k, (held0, held1))
    for b, chunk in enumerate((near, far)):
        scaled = chunk[...].astype(jnp.float32) * inverse[:, columns_of(k, dims)]
        block[b * rows : (b + 1) * rows, :] = scaled.astype(jnp.bfloat16)
    for side, out in enumerate((theirs, mine)):
        part = slice(side * half, (side + 1) * half)
        total = sums[part] + products(held[part, columns_of(k, dims, True)], block[...])
        near_out[part] = total[:, :rows]
        out[...] = total[:, rows:] * scale_of(factor, counts, half, side)


def near_kernel(k, side, factor, counts, held0, held1, inverse, last, near, *refs):
    out = refs[-1]
    half = out.shape[0]
    part = slice(side * half, (side + 1) * half)
    total = near[part] + one_product(k, part, (held0, held1), inverse, last)
    out[...] = total * scale_of(factor, counts, half, side)


def final_kernel(*refs):
    terms, out = refs[:-1], refs[-1]
    rows = terms[0].shape[1]
    for i in range(3):
        out[:, i * rows : (i + 1) * rows] = terms[2 * i][...] + terms[2 * i + 1][...]


def on_device(queries, documents, counts, eigenvalues):
    rows, dims = queries.shape
    doc_rows = documents.shape[0]
    half = doc_rows // 2
    owners = lax.axis_size("dp")
    factor = 1.0 / math.sqrt(dims * lax.axis_size("layer"))
    ahead = [(i, (i + 2) % owners) for i in range(owners)]
    pair = [(i, i ^ 1) for i in range(owners)]
    across = [(0, 1), (1, 0)]

    def chunk(k):
        return jax.ShapeDtypeStruct((rows, width_of(k, dims)), queries.dtype)

    def floats(*shape):
        return jax.ShapeDtypeStruct(shape, jnp.float32)

    def call(kernel, out_shape, in_specs, out_specs, scratch, vmem_mib=16, flops=PACE):
        return pl.pallas_call(
            kernel,
            out_shape=out_shape,
            in_specs=in_specs,
            out_specs=out_specs,
            scratch_shapes=scratch,
            compiler_params=pltpu.CompilerParams(vmem_limit_bytes=vmem_mib * MIB),
            cost_estimate=pl.CostEstimate(flops=flops, bytes_accessed=0, transcendentals=0),
        )

    def own_chunks(*ks, until=(), space=ANY, **options):
        return call(
            functools.partial(chunk_kernel, ks),
            [chunk(k) for k in ks],
            [ANY] * (1 + len(until)),
            [space] * len(ks),
            [pltpu.SemaphoreType.DMA((len(ks),))],
            **options,
        )(queries, *until)

    def step(k, *until):
        out = call(
            functools.partial(step_kernel, k),
            chunk(k),
            [ANY] * (2 + len(until)),
            ANY,
            [pltpu.SemaphoreType.DMA],
        )(queries, far[k], *until)
        near[k] = lax.ppermute(out, "dp", pair)
        return out

    def send_ahead(k, *until):
        (sent,) = own_chunks(k, until=until)
        far[k] = lax.ppermute(sent, "dp", ahead)
        return sent

    def pair_scores(*ks, sums=None, alone=None, until=()):
        operands = [*held, inverse] + [block[k] for k in ks for block in (near, far)]
        if sums is not None:
            operands.append(sums)
        if alone is not None:
            operands.append(far[alone])
        return call(
            functools.partial(pair_kernel, ks, alone, sums is None),
            floats(doc_rows, 2 * rows),
            [VMEM] * len(operands) + [ANY] * len(until),
            VMEM,
            [pltpu.VMEM((2 * rows, max(width_of(k, dims) for k in ks)), queries.dtype)],
        )(*operands, *until)

    def send_across(block, k, *until):
        sent = lax.optimization_barrier((block[k], *until))[0]
        block[CHUNKS - 1 - k] = lax.ppermute(sent, "groups", across)

    far = [None] * CHUNKS
    near = [None] * CHUNKS

    sent = own_chunks(0, space=VMEM, vmem_mib=53, flops=FIRST)
    far[0] = lax.ppermute(sent[0], "dp", ahead)
    sent += own_chunks(1, until=(sent[0],), space=VMEM)
    far[1] = lax.ppermute(sent[1], "dp", ahead)

    def own_scores(part, *operands, until=()):
        pieces = 4
        outs = [
            floats(half, rows),
            floats(half, rows),
            jax.ShapeDtypeStruct((doc_rows, dims // 2), documents.dtype),
            floats(1, dims),
        ][: 4 - part]
        return call(
            functools.partial(own_kernel, part, pieces, factor),
            outs,
            [SMEM, HBM] + [VMEM] * (1 + len(operands)) + [ANY] * len(until),
            [VMEM] * len(outs),
            [pltpu.SemaphoreType.DMA((pieces, 2))],
            vmem_mib=OWN_MIB[part],
        )(counts, documents, queries, *operands, *until)

    kept = lax.optimization_barrier((eigenvalues, sent[1]))[0].reshape(1, dims)
    theirs0, mine0, held0, inverse = own_scores(0, kept)

    out = step(0, inverse)
    out = send_ahead(2, out)
    send_across(far, 0, out)
    theirs0, mine0, held1 = own_scores(1, inverse, theirs0, mine0, until=(out,))
    held = held0, held1

    out = step(1, theirs0)
    out = send_ahead(3, out)
    send_across(near, 0, out)
    sums = pair_scores(0, until=(out, far[5]))

    out = step(2, sums)
    out = send_ahead(4, out)
    send_across(near, 1, out)
    sums = pair_scores(1, sums=sums, until=(out,))

    out = step(3, sums)
    got0 = lax.ppermute(lax.optimization_barrier((theirs0, out))[0], "layer", across)
    sums = pair_scores(2, 5, sums=sums, alone=3, until=(out,))
    near_sums, theirs_far, mine_far = call(
        functools.partial(far_kernel, 4, factor),
        [floats(doc_rows, rows), floats(half, rows), floats(half, rows)],
        [SMEM] + [VMEM] * 6,
        [VMEM] * 3,
        [pltpu.VMEM((2 * rows, width_of(4, dims)), queries.dtype)],
    )(counts, *held, inverse, near[4], far[4], sums)
    got_far = lax.ppermute(theirs_far, "layer", across)

    def near_scores(side, *until):
        return call(
            functools.partial(near_kernel, 3, side, factor),
            floats(half, rows),
            [SMEM] + [VMEM] * 5 + [ANY] * len(until),
            VMEM,
            [],
        )(counts, *held, inverse, near[3], near_sums, *until)

    theirs_near = near_scores(0, got0)
    got_near = lax.ppermute(theirs_near, "layer", across)
    mine_near = near_scores(1, theirs_near, got_far)
    return call(final_kernel, floats(half, 3 * rows), [VMEM] * 6, VMEM, [])(
        mine0, got0, mine_near, got_near, mine_far, got_far
    )


def solution(mesh):
    return jax.shard_map(
        on_device,
        mesh=mesh,
        in_specs=(P("dp", "layer"), P(("groups", "dp"), "layer"), P(("groups", "dp")), P("layer")),
        out_specs=P(("groups", "dp", "layer"), None),
        check_vma=False,
    )
```
